512 devices in a mesh: lo: 32 (over z, x_lo), hi: 16 (over x_hi, y, core).
Axes of the slice: x: 4 (x_hi: 2, x_lo: 2; x = x_hi * 2 + x_lo), y: 4, z: 16, core: 2. Of those that a mesh axis runs over, the one named last changes fastest.
Arguments:
- matrix: float32 [262144, 512], P(('lo', 'hi')), may hold values from -6 to 6
- sign_bits: int32 [2, 262144], P(None, ('lo', 'hi')), may hold values from 0 to 1
- sample_rows: int32 [65536], P(('lo', 'hi')), may hold values from 0 to 511
- sample_counts: int32 [512], P(('lo', 'hi')), may hold values from 64 to 128, as said below
Outputs:
- sketch: float32 [65536, 512], P(('lo', 'hi'))
- sketch_gram: float32 [512, 512], replicated
The draws below stay inside these ranges and needn't reach their ends.
Inputs may be any that keep to these rules, and one draw needn't show every extreme that they name: `sample_rows`: each entry is a row held by the same device as the slot, counted from that device's first row. `sample_counts`: slots at or past a device's count are unused; some device uses all 128 slots.
All inputs are finite; a program needn't handle non-finite values.
Results may differ from the reference program's by a relative error of at most 0.000098.
Values sent between devices are 32-bit elements; how exact they have to be, the bound alone decides.
A program may use at most 64 MiB of HBM per device.

```python
import math
import jax
import jax.numpy as jnp
from jax import lax

ROWS_DEV = 512
PANEL = 256
PANELS = 2
SLOTS = 128
WIDTH = 512
SHARDS = 512
ROWS = 262144


def draw_sample_counts(key, part):
    key = jax.random.fold_in(key, 7)
    first_key, second_key = jax.random.split(key)
    counts = jax.random.randint(first_key, (SHARDS,), SLOTS // 2, SLOTS + 1)
    position = jax.random.randint(second_key, (), 0, SHARDS)
    return jnp.where(jnp.arange(SHARDS) == position, SLOTS, counts).astype(jnp.int32)


def with_ends(drawn, own_key, least, top_value):
    longest = drawn.shape.index(max(drawn.shape))
    spots = []
    for shift in (0, 1):
        where = [jax.random.randint(jax.random.fold_in(own_key, axis), (), 0, length) for axis, length in enumerate(drawn.shape)]
        where[longest] = (where[longest] + shift) % drawn.shape[longest]
        spots.append(tuple(where))
    return drawn.at[spots[0]].set(least).at[spots[1]].set(top_value)


def steps_of(own_key, dims, cuts, least, largest):
    def one(dim, blocks):
        heights = jax.random.uniform(jax.random.fold_in(jax.random.fold_in(own_key, 6), dim), (blocks,), jnp.float32, least / len(cuts), largest / len(cuts))
        return jnp.repeat(jnp.exp(heights), dims[dim] // blocks).reshape((-1,) + (1,) * (len(dims) - dim - 1))

    level = one(*cuts[0])
    for cut in cuts[1:]:
        level = level * one(*cut)
    return level


def scatter_about(key, extent, scale, bound, pieces=(), kind=jnp.bfloat16):
    level = steps_of(key, extent, pieces, -0.22, 0.18) if pieces else 1.0
    entries = jax.random.normal(key, extent, jnp.float32) * scale * level
    return jnp.minimum(jnp.maximum(entries, -bound), bound).astype(kind)


def setup_inputs(seed: int = 0) -> dict:
    keys = jax.random.split(jax.random.key(seed), 5)
    return {
        "matrix": scatter_about(keys[0], (ROWS, WIDTH), 1.0, 6.0, ((0, 512),), jnp.float32),
        "sign_bits": with_ends(jax.random.randint(keys[1], (PANELS, ROWS), 0, 2), jax.random.fold_in(keys[1], 1), 0, 1).astype(jnp.int32),
        "sample_rows": with_ends(jax.random.randint(keys[2], (SHARDS * SLOTS,), 0, ROWS_DEV), jax.random.fold_in(keys[2], 1), 0, ROWS_DEV - 1).astype(jnp.int32),
        "sample_counts": draw_sample_counts(jax.random.fold_in(keys[4], 71), 0),
    }


def walsh_transform(values):
    total = values.shape[0]
    width = values.shape[1]
    for level in range(total.bit_length() - 1):
        stride = 2 ** level
        shaped = values.reshape(total // (2 * stride), 2, stride, width)
        upper = shaped[:, 0]
        lower = shaped[:, 1]
        values = jnp.stack([upper + lower, upper - lower], axis=1).reshape(total, width)
    return values

def reference(matrix, sign_bits, sample_rows, sample_counts):
    factors = (2 * sign_bits - 1).astype(jnp.float32).T
    signed = (matrix.reshape(ROWS, PANELS, PANEL) * factors[:, :, None]).reshape(ROWS, WIDTH)
    mixed = walsh_transform(signed) * (1.0 / math.sqrt(ROWS))
    blocks = mixed.reshape(SHARDS, ROWS_DEV, WIDTH)
    chosen = sample_rows.reshape(SHARDS, SLOTS).astype(jnp.int32)
    picked = jnp.take_along_axis(blocks, chosen[:, :, None], axis=1)
    live = (jnp.arange(SLOTS, dtype=jnp.int32)[None, :] < sample_counts[:, None]).astype(jnp.float32)
    sketch = (picked * live[:, :, None]).reshape(SHARDS * SLOTS, WIDTH)
    gram_sum = jnp.dot(sketch.T, sketch, precision=lax.Precision.HIGHEST, preferred_element_type=jnp.float32)
    return (sketch, gram_sum / (SHARDS * SLOTS))
```

```python
import functools
import math

import jax
import jax.numpy as jnp
from jax import lax
from jax.experimental import pallas as pl
from jax.experimental.pallas import tpu as pltpu
from jax.sharding import PartitionSpec as P

MESH = pl.DeviceIdType.MESH
LANES = 128


def parity_sign(value, bits):
    shift = 1
    while shift < bits:
        shift *= 2
    while shift > 1:
        shift //= 2
        value = jnp.bitwise_xor(value, jnp.right_shift(value, shift))
    return (1 - 2 * jnp.bitwise_and(value, 1)).astype(jnp.float32)


def kernel(
    geo, matrix_ref, bits_ref, rows_ref, count_ref, sketch_ref, gram_ref,
    signed, spread, back, whole, table, select, terms, ring, parts, gathered, sum_parts, z_low, z_high, mine,
    table_send, table_recv, out_send, out_recv, back_send, back_recv, ring_send, ring_recv, sum_send, sum_recv,
):
    size_z, size_x, size_hi = geo
    size_p = size_x * size_hi
    chunks = signed.shape[0]
    height = signed.shape[1] * signed.shape[2]
    slots = terms.shape[2]
    panels = bits_ref.shape[0]
    lo, hi = lax.axis_index("lo"), lax.axis_index("hi")
    z, x = lo // size_x, lo % size_x
    me = x * size_hi + hi

    def in_plane(step):
        peer = (me + step) % size_p
        return peer, (z * size_x + peer // size_hi, peer % size_hi)

    def on_ring(step):
        return (((z + step) % size_z) * size_x + x, hi)

    def wait_bytes(ref, sem):
        pltpu.make_async_copy(ref, ref, sem).wait()

    barrier = pltpu.get_barrier_semaphore()

    @pl.loop(1, size_p)
    def _(step):
        pl.semaphore_signal(barrier, inc=1, device_id=in_plane(step)[1], device_id_type=MESH)

    @pl.loop(1, size_z)
    def _(step):
        pl.semaphore_signal(barrier, inc=1, device_id=on_ring(step), device_id_type=MESH)

    factors = (2 * bits_ref[...] - 1).astype(jnp.float32)
    per_panel = chunks // panels
    for panel in range(panels):
        column = jnp.broadcast_to(factors[panel : panel + 1, :], (LANES, height)).T
        for chunk in range(panel * per_panel, (panel + 1) * per_panel):
            value = matrix_ref[:, chunk * LANES : (chunk + 1) * LANES] * column
            signed[chunk] = value.reshape(signed.shape[1:])
    lane = lax.broadcasted_iota(jnp.int32, (8, LANES), 1)
    picked = jnp.broadcast_to(rows_ref[...], (8, LANES))
    table[0] = jnp.where(lane < count_ref[0], picked, -1)

    pl.semaphore_wait(barrier, size_p - 1 + size_z - 1)

    @pl.loop(1, size_z)
    def _(step):
        pltpu.make_async_remote_copy(
            src_ref=table.at[0], dst_ref=table.at[step], send_sem=table_send.at[0], recv_sem=table_recv.at[0],
            device_id=on_ring(size_z - step), device_id_type=MESH,
        ).start()

    def send_out(chunk):
        @pl.loop(1, size_p)
        def _(step):
            peer, device = in_plane(step)
            pltpu.make_async_remote_copy(
                src_ref=signed.at[chunk, peer], dst_ref=spread.at[chunk, me],
                send_sem=out_send.at[chunk], recv_sem=out_recv.at[chunk],
                device_id=device, device_id_type=MESH,
            ).start()

        spread[chunk, me] = signed[chunk, me]

    def turn_back(chunk):
        wait_bytes(spread.at[chunk, pl.ds(0, size_p - 1)], out_recv.at[chunk])
        values = [spread[chunk, source] for source in range(size_p)]
        stride = 1
        while stride < size_p:
            values = [
                values[i] + values[i + stride] if i // stride % 2 == 0 else values[i - stride] - values[i]
                for i in range(size_p)
            ]
            stride *= 2
        for target in range(size_p):
            back[chunk, target] = values[target]

        @pl.loop(1, size_p)
        def _(step):
            peer, device = in_plane(step)
            pltpu.make_async_remote_copy(
                src_ref=back.at[chunk, peer], dst_ref=whole.at[chunk, me],
                send_sem=back_send.at[chunk], recv_sem=back_recv.at[chunk],
                device_id=device, device_id_type=MESH,
            ).start()

        whole[chunk, me] = back[chunk, me]

    def make_select():
        wait_bytes(table.at[pl.ds(1, size_z - 1)], table_recv.at[0])
        low = lax.broadcasted_iota(jnp.int32, (slots, LANES), 1)

        @pl.loop(0, size_z)
        def _(step):
            target = jnp.broadcast_to(table[step, 0:1, :].astype(jnp.float32), (LANES, slots)).T.astype(jnp.int32)
            sign = parity_sign(jnp.bitwise_and((z + step) % size_z, z), 4)
            base = parity_sign(jnp.bitwise_and(jnp.maximum(target, 0), low), 7)
            base = jnp.where(target < 0, 0.0, base * sign)
            blocks = [base]
            level = 7
            while len(blocks) * LANES < height:
                bit = jnp.bitwise_and(jnp.right_shift(jnp.maximum(target, 0), level), 1)
                flip = (1 - 2 * bit).astype(jnp.float32)
                blocks = blocks + [block * flip for block in blocks]
                level += 1
            for index, block in enumerate(blocks):
                select[step, :, index * LANES : (index + 1) * LANES] = block.astype(jnp.bfloat16)

    def make_terms(chunk):
        wait_bytes(whole.at[chunk, pl.ds(0, size_p - 1)], back_recv.at[chunk])
        value = whole[chunk].reshape(height, LANES)
        high = value.astype(jnp.bfloat16)
        rest = (value - high.astype(jnp.float32)).astype(jnp.bfloat16)
        both = jnp.concatenate([high, rest], axis=1)
        group = 4

        @pl.loop(0, size_z // group)
        def _(step):
            some = select[pl.ds(step * group, group)].reshape(group * slots, height)
            product = jnp.dot(some, both, preferred_element_type=jnp.float32)
            total = product[:, :LANES] + product[:, LANES:]
            terms[chunk, pl.ds(step * group, group)] = total.reshape(group, slots, LANES)

    half = size_z // 2

    def ways(chunk):
        longer = chunk * 2 < chunks
        right = [(half if longer else half - 1) - i for i in range(half if longer else half - 1)]
        left = [(half + 1 if longer else half) + i for i in range(half - 1 if longer else half)]
        return right, left

    def ring_copy(chunk, way, step, term):
        return pltpu.make_async_remote_copy(
            src_ref=terms.at[chunk, term], dst_ref=ring.at[chunk, way, step],
            send_sem=ring_send.at[chunk, way, step], recv_sem=ring_recv.at[chunk, way, step],
            device_id=on_ring(1 if way == 0 else size_z - 1), device_id_type=MESH,
        )

    sent = []

    def ring_step(chunk, step):
        for way, targets in enumerate(ways(chunk)):
            if step > len(targets):
                continue
            term = targets[step] if step < len(targets) else 0
            if step > 0:
                ring_copy(chunk, way, step - 1, term).wait_recv()
                terms[chunk, term] = terms[chunk, term] + ring[chunk, way, step - 1]
            if step < len(targets):
                copy = ring_copy(chunk, way, step, term)
                copy.start()
                sent.append(copy)

    send_out(0)
    send_out(1)
    make_select()
    turn_back(0)
    send_out(2)
    turn_back(1)
    send_out(3)
    make_terms(0)
    ring_step(0, 0)
    turn_back(2)
    make_terms(1)
    ring_step(1, 0)
    ring_step(0, 1)
    turn_back(3)
    make_terms(2)
    ring_step(2, 0)
    ring_step(0, 2)
    ring_step(1, 1)
    make_terms(3)
    ring_step(3, 0)
    for turn in range(1, half + 3):
        ring_step(0, turn + 2)
        ring_step(1, turn + 1)
        ring_step(2, turn)
        ring_step(3, turn)

    scale = 1.0 / math.sqrt(height * size_p * size_z)
    pieces = [terms[chunk, 0] * scale for chunk in range(chunks)]
    for chunk in range(chunks):
        sketch_ref[:, chunk * LANES : (chunk + 1) * LANES] = pieces[chunk]
    sketch = jnp.concatenate(pieces, axis=1)
    block = 0
    for i in range(chunks):
        product = jnp.dot(
            pieces[i].T, sketch[:, i * LANES :], precision=lax.Precision.HIGHEST, preferred_element_type=jnp.float32
        )
        for j in range(chunks - i):
            parts[block * LANES : (block + 1) * LANES, :] = product[:, j * LANES : (j + 1) * LANES]
            block += 1

    deep = sum_parts.shape[1]

    @pl.loop(1, size_p)
    def _(step):
        peer, device = in_plane(step)
        pltpu.make_async_remote_copy(
            src_ref=parts.at[pl.ds(pl.multiple_of(peer * deep, 8), deep)], dst_ref=sum_parts.at[step - 1],
            send_sem=sum_send.at[0], recv_sem=sum_recv.at[0], device_id=device, device_id_type=MESH,
        ).start()

    total = parts[pl.ds(pl.multiple_of(me * deep, 8), deep), :]
    wait_bytes(sum_parts, sum_recv.at[0])
    for step in range(size_p - 1):
        total = total + sum_parts[step]

    low_size, high_size = z_low.shape[0], z_high.shape[0]
    z_lo, z_hi = z % low_size, z // low_size
    z_low[z_lo] = total
    for step in range(1, low_size):
        peer = z_hi * low_size + (z_lo + step) % low_size
        pltpu.make_async_remote_copy(
            src_ref=z_low.at[z_lo], dst_ref=z_low.at[z_lo], send_sem=sum_send.at[1], recv_sem=sum_recv.at[1],
            device_id=(peer * size_x + x, hi), device_id_type=MESH,
        ).start()
    wait_bytes(z_low.at[pl.ds(0, low_size - 1)], sum_recv.at[1])
    total = z_low[0]
    for step in range(1, low_size):
        total = total + z_low[step]
    z_high[z_hi] = total
    for step in range(1, high_size):
        peer = ((z_hi + step) % high_size) * low_size + z_lo
        pltpu.make_async_remote_copy(
            src_ref=z_high.at[z_hi], dst_ref=z_high.at[z_hi], send_sem=sum_send.at[2], recv_sem=sum_recv.at[2],
            device_id=(peer * size_x + x, hi), device_id_type=MESH,
        ).start()
    if high_size > 1:
        wait_bytes(z_high.at[pl.ds(0, high_size - 1)], sum_recv.at[2])
    total = z_high[0]
    for step in range(1, high_size):
        total = total + z_high[step]
    mine[...] = total * (1.0 / (size_p * size_z * slots))
    own = pl.ds(pl.multiple_of(me * deep, 8), deep)

    @pl.loop(1, size_p)
    def _(step):
        pltpu.make_async_remote_copy(
            src_ref=mine, dst_ref=gathered.at[own], send_sem=sum_send.at[3], recv_sem=sum_recv.at[3],
            device_id=in_plane(step)[1], device_id_type=MESH,
        ).start()

    gathered[own, :] = mine[...]
    wait_bytes(gathered.at[pl.ds(0, deep * (size_p - 1))], sum_recv.at[3])
    block = 0
    for i in range(chunks):
        for j in range(i, chunks):
            value = gathered[block * LANES : (block + 1) * LANES, :]
            gram_ref[i * LANES : (i + 1) * LANES, j * LANES : (j + 1) * LANES] = value
            if j > i:
                gram_ref[j * LANES : (j + 1) * LANES, i * LANES : (i + 1) * LANES] = value.T
            block += 1

    for copy in sent:
        copy.wait_send()
    wait_bytes(table.at[pl.ds(1, size_z - 1)], table_send.at[0])
    for chunk in range(chunks):
        wait_bytes(signed.at[chunk, pl.ds(0, size_p - 1)], out_send.at[chunk])
        wait_bytes(back.at[chunk, pl.ds(0, size_p - 1)], back_send.at[chunk])
    wait_bytes(sum_parts, sum_send.at[0])
    wait_bytes(z_low.at[pl.ds(0, low_size - 1)], sum_send.at[1])
    if high_size > 1:
        wait_bytes(z_high.at[pl.ds(0, high_size - 1)], sum_send.at[2])
    wait_bytes(gathered.at[pl.ds(0, deep * (size_p - 1))], sum_send.at[3])


def build(geo, matrix, sign_bits, sample_rows, sample_counts):
    size_z, size_x, size_hi = geo
    size_p = size_x * size_hi
    height, width = matrix.shape
    slots = sample_rows.shape[0]
    chunks = width // LANES
    packed = chunks * (chunks + 1) // 2 * LANES
    deep = packed // size_p
    low_size = 4
    f32 = jnp.float32
    vmem = pl.BlockSpec(memory_space=pltpu.VMEM)
    dma = pltpu.SemaphoreType.DMA
    spread = (chunks, size_p, height // size_p, LANES)
    return pl.pallas_call(
        functools.partial(kernel, geo),
        out_shape=(
            jax.ShapeDtypeStruct((slots, width), f32),
            jax.ShapeDtypeStruct((width, width), f32),
        ),
        in_specs=[vmem, vmem, vmem, pl.BlockSpec(memory_space=pltpu.SMEM)],
        out_specs=(vmem, vmem),
        scratch_shapes=[
            pltpu.VMEM(spread, f32),
            pltpu.VMEM(spread, f32),
            pltpu.VMEM(spread, f32),
            pltpu.VMEM(spread, f32),
            pltpu.VMEM((size_z, 8, LANES), jnp.int32),
            pltpu.VMEM((size_z, slots, height), jnp.bfloat16),
            pltpu.VMEM((chunks, size_z, slots, LANES), f32),
            pltpu.VMEM((chunks, 2, size_z // 2, slots, LANES), f32),
            pltpu.VMEM((packed, LANES), f32),
            pltpu.VMEM((packed, LANES), f32),
            pltpu.VMEM((size_p - 1, deep, LANES), f32),
            pltpu.VMEM((low_size, deep, LANES), f32),
            pltpu.VMEM((size_z // low_size, deep, LANES), f32),
            pltpu.VMEM((deep, LANES), f32),
            dma((1,)),
            dma((1,)),
            dma((chunks,)),
            dma((chunks,)),
            dma((chunks,)),
            dma((chunks,)),
            dma((chunks, 2, size_z // 2)),
            dma((chunks, 2, size_z // 2)),
            dma((4,)),
            dma((4,)),
        ],
        compiler_params=pltpu.CompilerParams(
            collective_id=0, has_side_effects=True, vmem_limit_bytes=48 * 1024 * 1024
        ),
    )(matrix, sign_bits, sample_rows.reshape(1, slots), sample_counts)


def solution(mesh):
    size_x = 2
    geo = (mesh.shape["lo"] // size_x, size_x, mesh.shape["hi"])
    in_specs = (P(("lo", "hi"), None), P(None, ("lo", "hi")), P(("lo", "hi")), P(("lo", "hi")))
    out_specs = (P(("lo", "hi"), None), P())
    return jax.shard_map(
        functools.partial(build, geo), mesh=mesh, in_specs=in_specs, out_specs=out_specs, check_vma=False
    )
```

```python
import functools
import math

import jax
import jax.numpy as jnp
from jax import lax
from jax.experimental import pallas as pl
from jax.experimental.pallas import tpu as pltpu
from jax.sharding import PartitionSpec as P

MESH = pl.DeviceIdType.MESH
LANES = 128


def parity_sign(value, bits):
    shift = 1
    while shift < bits:
        shift *= 2
    while shift > 1:
        shift //= 2
        value = jnp.bitwise_xor(value, jnp.right_shift(value, shift))
    return (1 - 2 * jnp.bitwise_and(value, 1)).astype(jnp.float32)


def butterflies(values):
    stride = 1
    while stride < len(values):
        values = [
            values[i] + values[i + stride] if i // stride % 2 == 0 else values[i - stride] - values[i]
            for i in range(len(values))
        ]
        stride *= 2
    return values


def kernel(
    geo, matrix_ref, bits_ref, rows_ref, count_ref, sketch_ref, gram_ref,
    raw, bits, rows, signed, other, mixed, spread, back, whole, table, select, terms, ring,
    turned, turned_in, turned_mid, turned_other, turned_mix, turned_spread, turned_back, turned_whole, turned_out,
    turned_final, parts, half_parts, sum_parts, z_low, z_high, gathered,
    load_sem, core_send, core_recv, table_send, table_recv, out_send, out_recv, back_send, back_recv,
    ring_send, ring_recv, sum_send, sum_recv, turn_send, turn_recv,
):
    size_z, size_x, size_hi = geo
    cores = 2
    size_y = size_hi // cores
    size_p = size_x * size_y
    chunks = raw.shape[0]
    rounds = chunks - 1
    height = signed.shape[1]
    slots = terms.shape[2]
    panels = bits.shape[0]
    lo, hi = lax.axis_index("lo"), lax.axis_index("hi")
    z, x = lo // size_x, lo % size_x
    core = hi % cores
    me = x * size_y + hi // cores
    twin = (lo, hi + 1 - 2 * core)

    def in_plane(step):
        peer = (me + step) % size_p
        return peer, (z * size_x + peer // size_y, (peer % size_y) * cores + core)

    def on_ring(step):
        return (((z + step) % size_z) * size_x + x, hi)

    def wait_bytes(ref, sem):
        pltpu.make_async_copy(ref, ref, sem).wait()

    barrier = pltpu.get_barrier_semaphore()
    pl.semaphore_signal(barrier, inc=1, device_id=twin, device_id_type=MESH)

    @pl.loop(1, size_p)
    def _(step):
        pl.semaphore_signal(barrier, inc=1, device_id=in_plane(step)[1], device_id_type=MESH)

    @pl.loop(1, size_z)
    def _(step):
        pl.semaphore_signal(barrier, inc=1, device_id=on_ring(step), device_id_type=MESH)

    loads = [pltpu.make_async_copy(bits_ref, bits, load_sem.at[chunks])]
    for chunk in range(chunks):
        loads.append(pltpu.make_async_copy(
            matrix_ref.at[:, chunk * LANES : (chunk + 1) * LANES], raw.at[chunk], load_sem.at[chunk]
        ))
    loads.append(pltpu.make_async_copy(rows_ref, rows, load_sem.at[chunks + 1]))
    for load in loads:
        load.start()

    loads[0].wait()
    factors = (2 * bits[...] - 1).astype(jnp.float32)
    columns = [jnp.broadcast_to(factors[p : p + 1, :], (LANES, height)).T for p in range(panels)]

    def twin_copy(chunk):
        return pltpu.make_async_remote_copy(
            src_ref=signed.at[chunk], dst_ref=other.at[chunk], send_sem=core_send.at[chunk],
            recv_sem=core_recv.at[chunk], device_id=twin, device_id_type=MESH,
        )

    def sign(chunk):
        loads[1 + chunk].wait()
        return raw[chunk] * columns[chunk * panels // chunks]

    signed[0] = sign(0)
    turned[...] = sign(rounds).T.reshape(turned.shape)
    pl.semaphore_wait(barrier, 1 + size_p - 1 + size_z - 1)
    twin_copy(0).start()

    def along_z(source, target, index):
        @pl.loop(1, size_z)
        def _(step):
            peer = (z + step) % size_z
            pltpu.make_async_remote_copy(
                src_ref=source.at[peer], dst_ref=target.at[z], send_sem=turn_send.at[index],
                recv_sem=turn_recv.at[index], device_id=on_ring(step), device_id_type=MESH,
            ).start()

        target[z] = source[z]

    along_z(turned, turned_in, 0)
    loads[-1].wait()
    lane = lax.broadcasted_iota(jnp.int32, (8, LANES), 1)
    table[0] = jnp.where(lane < count_ref[0], jnp.broadcast_to(rows[...], (8, LANES)), -1)

    @pl.loop(1, size_z)
    def _(step):
        pltpu.make_async_remote_copy(
            src_ref=table.at[0], dst_ref=table.at[step], send_sem=table_send.at[0], recv_sem=table_recv.at[0],
            device_id=on_ring(size_z - step), device_id_type=MESH,
        ).start()

    for chunk in range(1, rounds):
        signed[chunk] = sign(chunk)
        twin_copy(chunk).start()

    own_sign = (1 - 2 * core).astype(jnp.float32)

    def send_out(chunk):
        twin_copy(chunk).wait_recv()
        mixed[chunk] = (signed[chunk] * own_sign + other[chunk]).reshape(mixed.shape[1:])

        @pl.loop(1, size_p)
        def _(step):
            peer, device = in_plane(step)
            pltpu.make_async_remote_copy(
                src_ref=mixed.at[chunk, peer], dst_ref=spread.at[chunk, me],
                send_sem=out_send.at[chunk], recv_sem=out_recv.at[chunk],
                device_id=device, device_id_type=MESH,
            ).start()

        spread[chunk, me] = mixed[chunk, me]

    def turn_back(chunk):
        wait_bytes(spread.at[chunk, pl.ds(0, size_p - 1)], out_recv.at[chunk])
        values = butterflies([spread[chunk, source] for source in range(size_p)])
        for target in range(size_p):
            back[chunk, target] = values[target]

        @pl.loop(1, size_p)
        def _(step):
            peer, device = in_plane(step)
            pltpu.make_async_remote_copy(
                src_ref=back.at[chunk, peer], dst_ref=whole.at[chunk, me],
                send_sem=back_send.at[chunk], recv_sem=back_recv.at[chunk],
                device_id=device, device_id_type=MESH,
            ).start()

        whole[chunk, me] = back[chunk, me]

    def z_sign(step):
        return parity_sign(jnp.bitwise_and((z + step) % size_z, z), 4)

    def make_select():
        wait_bytes(table.at[pl.ds(1, size_z - 1)], table_recv.at[0])
        low = lax.broadcasted_iota(jnp.int32, (slots, LANES), 1)

        @pl.loop(0, size_z)
        def _(step):
            target = jnp.broadcast_to(table[step, 0:1, :].astype(jnp.float32), (LANES, slots)).T.astype(jnp.int32)
            sign = z_sign(step)
            base = parity_sign(jnp.bitwise_and(jnp.maximum(target, 0), low), 7)
            base = jnp.where(target < 0, 0.0, base * sign)
            blocks = [base]
            level = 7
            while len(blocks) * LANES < height:
                bit = jnp.bitwise_and(jnp.right_shift(jnp.maximum(target, 0), level), 1)
                flip = (1 - 2 * bit).astype(jnp.float32)
                blocks = blocks + [block * flip for block in blocks]
                level += 1
            for index, block in enumerate(blocks):
                select[step, :, index * LANES : (index + 1) * LANES] = block.astype(jnp.bfloat16)

    def make_terms(chunk):
        wait_bytes(whole.at[chunk, pl.ds(0, size_p - 1)], back_recv.at[chunk])
        value = whole[chunk].reshape(height, LANES)
        high = value.astype(jnp.bfloat16)
        rest = (value - high.astype(jnp.float32)).astype(jnp.bfloat16)
        both = jnp.concatenate([high, rest], axis=1)
        group = 4

        @pl.loop(0, size_z // group)
        def _(step):
            some = select[pl.ds(step * group, group)].reshape(group * slots, height)
            product = jnp.dot(some, both, preferred_element_type=jnp.float32)
            total = product[:, :LANES] + product[:, LANES:]
            terms[chunk, pl.ds(step * group, group)] = total.reshape(group, slots, LANES)

    half = size_z // 2

    def ways(chunk):
        longer = chunk % 2 == 0
        right = [(half if longer else half - 1) - i for i in range(half if longer else half - 1)]
        left = [(half + 1 if longer else half) + i for i in range(half - 1 if longer else half)]
        return right, left

    def ring_copy(chunk, way, step, term):
        return pltpu.make_async_remote_copy(
            src_ref=terms.at[chunk, term], dst_ref=ring.at[chunk, way, step],
            send_sem=ring_send.at[chunk, way, step], recv_sem=ring_recv.at[chunk, way, step],
            device_id=on_ring(1 if way == 0 else size_z - 1), device_id_type=MESH,
        )

    sent = []

    def ring_step(chunk, step):
        for way, targets in enumerate(ways(chunk)):
            if step > len(targets):
                continue
            term = targets[step] if step < len(targets) else 0
            if step > 0:
                ring_copy(chunk, way, step - 1, term).wait_recv()
                terms[chunk, term] = terms[chunk, term] + ring[chunk, way, step - 1]
            if step < len(targets):
                copy = ring_copy(chunk, way, step, term)
                copy.start()
                sent.append(copy)

    each = size_z // size_p

    def turned_to_plane():
        wait_bytes(turned_in.at[pl.ds(0, size_z - 1)], turn_recv.at[0])
        for target, value in enumerate(butterflies([turned_in[source] for source in range(size_z)])):
            turned_mid[target] = value
        turned_twin.start()
        turned_twin.wait_recv()
        turned_mix[...] = turned_mid[...] * own_sign + turned_other[...]

        @pl.loop(1, size_p)
        def _(step):
            peer, device = in_plane(step)
            pltpu.make_async_remote_copy(
                src_ref=turned_mix.at[pl.ds(peer * each, each)], dst_ref=turned_spread.at[me],
                send_sem=turn_send.at[2], recv_sem=turn_recv.at[2], device_id=device, device_id_type=MESH,
            ).start()

        turned_spread[me] = turned_mix[pl.ds(me * each, each)]

    def turned_from_plane():
        wait_bytes(turned_spread.at[pl.ds(0, size_p - 1)], turn_recv.at[2])
        for target, value in enumerate(butterflies([turned_spread[source] for source in range(size_p)])):
            turned_back[target] = value

        @pl.loop(1, size_p)
        def _(step):
            peer, device = in_plane(step)
            pltpu.make_async_remote_copy(
                src_ref=turned_back.at[peer], dst_ref=turned_whole.at[pl.ds(me * each, each)],
                send_sem=turn_send.at[3], recv_sem=turn_recv.at[3], device_id=device, device_id_type=MESH,
            ).start()

        turned_whole[pl.ds(me * each, each)] = turned_back[me]

    def turned_select():
        wait_bytes(turned_whole.at[pl.ds(0, each * (size_p - 1))], turn_recv.at[3])
        deep = turned.shape[1]

        @pl.loop(0, size_z)
        def _(step):
            peer = (z + step) % size_z
            value = turned_whole[peer]
            high = value.astype(jnp.bfloat16).astype(jnp.float32)
            both = jnp.concatenate([high, value - high], axis=0).astype(jnp.bfloat16)
            product = lax.dot_general(
                both, select[step], (((1,), (1,)), ((), ())), preferred_element_type=jnp.float32
            )
            turned_out[peer] = (product[:deep] + product[deep:]) * z_sign(step)

        along_z(turned_out, turned_final, 4)

    turned_twin = pltpu.make_async_remote_copy(
        src_ref=turned_mid, dst_ref=turned_other, send_sem=turn_send.at[1], recv_sem=turn_recv.at[1],
        device_id=twin, device_id_type=MESH,
    )

    for chunk in range(rounds):
        send_out(chunk)
    turn_back(0)
    make_select()
    turn_back(1)
    turn_back(2)
    make_terms(0)
    ring_step(0, 0)
    turned_to_plane()
    make_terms(1)
    ring_step(1, 0)
    ring_step(0, 1)
    make_terms(2)
    ring_step(2, 0)
    ring_step(0, 2)
    ring_step(1, 1)
    turned_from_plane()
    ring_step(2, 1)
    ring_step(0, 3)
    ring_step(1, 2)
    ring_step(2, 2)
    ring_step(0, 4)
    ring_step(1, 3)
    turned_select()
    for turn in range(3, half + 1):
        ring_step(2, turn)
        ring_step(0, turn + 2)
        ring_step(1, turn + 1)
    wait_bytes(turned_final.at[pl.ds(0, size_z - 1)], turn_recv.at[4])

    scale = 1.0 / math.sqrt(height * size_p * cores * size_z)
    pieces = [terms[chunk, 0] * scale for chunk in range(rounds)]
    pieces.append(turned_final[...].reshape(LANES, slots).T * scale)
    for chunk in range(chunks):
        sketch_ref[:, chunk * LANES : (chunk + 1) * LANES] = pieces[chunk]
    sketch = jnp.concatenate(pieces, axis=1)
    block = 0
    for i in range(chunks):
        product = jnp.dot(
            pieces[i].T, sketch[:, i * LANES :], precision=lax.Precision.HIGHEST, preferred_element_type=jnp.float32
        )
        for j in range(chunks - i):
            parts[block * LANES : (block + 1) * LANES, :] = product[:, j * LANES : (j + 1) * LANES]
            block += 1

    deep = sum_parts.shape[1]
    share = deep * size_p

    def twin_half(source, first, target, sem):
        return pltpu.make_async_remote_copy(
            src_ref=source.at[pl.ds(first, share)], dst_ref=target, send_sem=sum_send.at[sem],
            recv_sem=sum_recv.at[sem], device_id=twin, device_id_type=MESH,
        )

    mine = pl.multiple_of(core * share, 8)
    yours = pl.multiple_of((1 - core) * share, 8)
    first_swap = twin_half(parts, yours, half_parts, 0)
    first_swap.start()
    first_swap.wait_recv()
    half_parts[...] = half_parts[...] + parts[pl.ds(mine, share), :]

    @pl.loop(1, size_p)
    def _(step):
        peer, device = in_plane(step)
        pltpu.make_async_remote_copy(
            src_ref=half_parts.at[pl.ds(pl.multiple_of(peer * deep, 8), deep)], dst_ref=sum_parts.at[step - 1],
            send_sem=sum_send.at[1], recv_sem=sum_recv.at[1], device_id=device, device_id_type=MESH,
        ).start()

    total = half_parts[pl.ds(pl.multiple_of(me * deep, 8), deep), :]
    wait_bytes(sum_parts, sum_recv.at[1])
    for step in range(size_p - 1):
        total = total + sum_parts[step]

    low_size, high_size = z_low.shape[0], z_high.shape[0]
    z_lo, z_hi = z % low_size, z // low_size
    z_low[z_lo] = total
    for step in range(1, low_size):
        peer = z_hi * low_size + (z_lo + step) % low_size
        pltpu.make_async_remote_copy(
            src_ref=z_low.at[z_lo], dst_ref=z_low.at[z_lo], send_sem=sum_send.at[2], recv_sem=sum_recv.at[2],
            device_id=(peer * size_x + x, hi), device_id_type=MESH,
        ).start()
    wait_bytes(z_low.at[pl.ds(0, low_size - 1)], sum_recv.at[2])
    total = z_low[0]
    for step in range(1, low_size):
        total = total + z_low[step]
    z_high[z_hi] = total
    for step in range(1, high_size):
        peer = ((z_hi + step) % high_size) * low_size + z_lo
        pltpu.make_async_remote_copy(
            src_ref=z_high.at[z_hi], dst_ref=z_high.at[z_hi], send_sem=sum_send.at[3], recv_sem=sum_recv.at[3],
            device_id=(peer * size_x + x, hi), device_id_type=MESH,
        ).start()
    if high_size > 1:
        wait_bytes(z_high.at[pl.ds(0, high_size - 1)], sum_recv.at[3])
    total = z_high[0]
    for step in range(1, high_size):
        total = total + z_high[step]
    own = pl.ds(pl.multiple_of(core * share + me * deep, 8), deep)
    gathered[own, :] = total * (1.0 / (size_p * cores * size_z * slots))

    @pl.loop(1, size_p)
    def _(step):
        pltpu.make_async_remote_copy(
            src_ref=gathered.at[own], dst_ref=gathered.at[own], send_sem=sum_send.at[4], recv_sem=sum_recv.at[4],
            device_id=in_plane(step)[1], device_id_type=MESH,
        ).start()

    rest = pl.ds(0, deep * (size_p - 1))
    wait_bytes(gathered.at[rest], sum_recv.at[4])
    last_swap = twin_half(gathered, mine, gathered.at[pl.ds(mine, share)], 5)
    last_swap.start()
    last_swap.wait_recv()
    block = 0
    for i in range(chunks):
        for j in range(i, chunks):
            value = gathered[block * LANES : (block + 1) * LANES, :]
            gram_ref[i * LANES : (i + 1) * LANES, j * LANES : (j + 1) * LANES] = value
            if j > i:
                gram_ref[j * LANES : (j + 1) * LANES, i * LANES : (i + 1) * LANES] = value.T
            block += 1

    for copy in sent:
        copy.wait_send()
    wait_bytes(table.at[pl.ds(1, size_z - 1)], table_send.at[0])
    turned_twin.wait_send()
    wait_bytes(turned_in.at[pl.ds(0, size_z - 1)], turn_send.at[0])
    wait_bytes(turned_mix.at[pl.ds(0, each * (size_p - 1))], turn_send.at[2])
    wait_bytes(turned_back.at[pl.ds(0, size_p - 1)], turn_send.at[3])
    wait_bytes(turned_final.at[pl.ds(0, size_z - 1)], turn_send.at[4])
    for chunk in range(rounds):
        twin_copy(chunk).wait_send()
        wait_bytes(mixed.at[chunk, pl.ds(0, size_p - 1)], out_send.at[chunk])
        wait_bytes(back.at[chunk, pl.ds(0, size_p - 1)], back_send.at[chunk])
    first_swap.wait_send()
    wait_bytes(sum_parts, sum_send.at[1])
    wait_bytes(z_low.at[pl.ds(0, low_size - 1)], sum_send.at[2])
    if high_size > 1:
        wait_bytes(z_high.at[pl.ds(0, high_size - 1)], sum_send.at[3])
    wait_bytes(gathered.at[rest], sum_send.at[4])
    last_swap.wait_send()


def build(geo, matrix, sign_bits, sample_rows, sample_counts):
    size_z, size_x, size_hi = geo
    cores = 2
    size_p = size_x * size_hi // cores
    height, width = matrix.shape
    slots = sample_rows.shape[0]
    chunks = width // LANES
    packed = chunks * (chunks + 1) // 2 * LANES
    deep = packed // cores // size_p
    low_size = 4
    f32 = jnp.float32
    vmem = pl.BlockSpec(memory_space=pltpu.VMEM)
    hbm = pl.BlockSpec(memory_space=pltpu.HBM)
    dma = pltpu.SemaphoreType.DMA
    rounds = chunks - 1
    tall = (rounds, height, LANES)
    spread = (rounds, size_p, height // size_p, LANES)
    turned = (size_z, LANES // size_z, height)
    turned_spread = (size_p, size_z // size_p, LANES // size_z, height)
    turned_out = (size_z, LANES // size_z, slots)
    return pl.pallas_call(
        functools.partial(kernel, geo),
        out_shape=(
            jax.ShapeDtypeStruct((slots, width), f32),
            jax.ShapeDtypeStruct((width, width), f32),
        ),
        in_specs=[hbm, hbm, hbm, pl.BlockSpec(memory_space=pltpu.SMEM)],
        out_specs=(vmem, vmem),
        scratch_shapes=[
            pltpu.VMEM((chunks, height, LANES), f32),
            pltpu.VMEM(sign_bits.shape, jnp.int32),
            pltpu.VMEM((1, slots), jnp.int32),
            pltpu.VMEM(tall, f32),
            pltpu.VMEM(tall, f32),
            pltpu.VMEM(spread, f32),
            pltpu.VMEM(spread, f32),
            pltpu.VMEM(spread, f32),
            pltpu.VMEM(spread, f32),
            pltpu.VMEM((size_z, 8, LANES), jnp.int32),
            pltpu.VMEM((size_z, slots, height), jnp.bfloat16),
            pltpu.VMEM((rounds, size_z, slots, LANES), f32),
            pltpu.VMEM((rounds, 2, size_z // 2, slots, LANES), f32),
            pltpu.VMEM(turned, f32),
            pltpu.VMEM(turned, f32),
            pltpu.VMEM(turned, f32),
            pltpu.VMEM(turned, f32),
            pltpu.VMEM(turned, f32),
            pltpu.VMEM(turned_spread, f32),
            pltpu.VMEM(turned_spread, f32),
            pltpu.VMEM(turned, f32),
            pltpu.VMEM(turned_out, f32),
            pltpu.VMEM(turned_out, f32),

            pltpu.VMEM((packed, LANES), f32),
            pltpu.VMEM((packed // cores, LANES), f32),
            pltpu.VMEM((size_p - 1, deep, LANES), f32),
            pltpu.VMEM((low_size, deep, LANES), f32),
            pltpu.VMEM((size_z // low_size, deep, LANES), f32),
            pltpu.VMEM((packed, LANES), f32),
            dma((chunks + 2,)),
            dma((rounds,)),
            dma((rounds,)),
            dma((1,)),
            dma((1,)),
            dma((rounds,)),
            dma((rounds,)),
            dma((rounds,)),
            dma((rounds,)),
            dma((rounds, 2, size_z // 2)),
            dma((rounds, 2, size_z // 2)),
            dma((6,)),
            dma((6,)),
            dma((5,)),
            dma((5,)),
        ],
        compiler_params=pltpu.CompilerParams(
            collective_id=0, has_side_effects=True, vmem_limit_bytes=48 * 1024 * 1024
        ),
    )(matrix, sign_bits, sample_rows.reshape(1, slots), sample_counts)


def solution(mesh):
    size_x = 2
    geo = (mesh.shape["lo"] // size_x, size_x, mesh.shape["hi"])
    in_specs = (P(("lo", "hi"), None), P(None, ("lo", "hi")), P(("lo", "hi")), P(("lo", "hi")))
    out_specs = (P(("lo", "hi"), None), P())
    return jax.shard_map(
        functools.partial(build, geo), mesh=mesh, in_specs=in_specs, out_specs=out_specs, check_vma=False
    )
```

```python
import functools
import math

import jax
import jax.numpy as jnp
from jax import lax
from jax.experimental import pallas as pl
from jax.experimental.pallas import tpu as pltpu
from jax.sharding import PartitionSpec as P

MESH = pl.DeviceIdType.MESH
LANES = 128


def parity_sign(value, bits):
    shift = 1
    while shift < bits:
        shift *= 2
    while shift > 1:
        shift //= 2
        value = jnp.bitwise_xor(value, jnp.right_shift(value, shift))
    return (1 - 2 * jnp.bitwise_and(value, 1)).astype(jnp.float32)


def butterflies(values):
    stride = 1
    while stride < len(values):
        values = [
            values[i] + values[i + stride] if i // stride % 2 == 0 else values[i - stride] - values[i]
            for i in range(len(values))
        ]
        stride *= 2
    return values


def kernel(
    geo, matrix_ref, bits_ref, rows_ref, count_ref, sketch_ref, gram_ref,
    raw, bits, rows, signed, other, mixed, spread, back, whole, table, select, terms, ring,
    turned, turned_in, turned_mid, turned_other, turned_mix, turned_spread, turned_back, turned_whole, turned_out,
    turned_final, parts, half_parts, sum_parts, z_low, z_high, gathered,
    load_sem, core_send, core_recv, table_send, table_recv, out_send, out_recv, back_send, back_recv,
    ring_send, ring_recv, sum_send, sum_recv, turn_send, turn_recv,
):
    size_z, size_x, size_hi = geo
    cores = 2
    size_y = size_hi // cores
    size_p = size_x * size_y
    chunks = raw.shape[0]
    rounds = chunks - 1
    height = signed.shape[1]
    slots = terms.shape[2]
    panels = bits.shape[0]
    lo, hi = lax.axis_index("lo"), lax.axis_index("hi")
    z, x = lo // size_x, lo % size_x
    core = hi % cores
    me = x * size_y + hi // cores
    twin = (lo, hi + 1 - 2 * core)

    def in_plane(step):
        peer = (me + step) % size_p
        return peer, (z * size_x + peer // size_y, (peer % size_y) * cores + core)

    def on_ring(step):
        return (((z + step) % size_z) * size_x + x, hi)

    def wait_bytes(ref, sem):
        pltpu.make_async_copy(ref, ref, sem).wait()

    barrier = pltpu.get_barrier_semaphore()
    pl.semaphore_signal(barrier, inc=1, device_id=twin, device_id_type=MESH)

    @pl.loop(1, size_p)
    def _(step):
        pl.semaphore_signal(barrier, inc=1, device_id=in_plane(step)[1], device_id_type=MESH)

    @pl.loop(1, size_z)
    def _(step):
        pl.semaphore_signal(barrier, inc=1, device_id=on_ring(step), device_id_type=MESH)

    loads = [pltpu.make_async_copy(bits_ref, bits, load_sem.at[chunks])]
    for chunk in range(chunks):
        loads.append(pltpu.make_async_copy(
            matrix_ref.at[:, chunk * LANES : (chunk + 1) * LANES], raw.at[chunk], load_sem.at[chunk]
        ))
    loads.append(pltpu.make_async_copy(rows_ref, rows, load_sem.at[chunks + 1]))
    for load in loads:
        load.start()

    loads[0].wait()
    factors = (2 * bits[...] - 1).astype(jnp.float32)
    columns = [jnp.broadcast_to(factors[p : p + 1, :], (LANES, height)).T for p in range(panels)]

    def twin_copy(chunk):
        return pltpu.make_async_remote_copy(
            src_ref=signed.at[chunk], dst_ref=other.at[chunk], send_sem=core_send.at[chunk],
            recv_sem=core_recv.at[chunk], device_id=twin, device_id_type=MESH,
        )

    def sign(chunk):
        loads[1 + chunk].wait()
        return raw[chunk] * columns[chunk * panels // chunks]

    signed[0] = sign(0)
    pl.semaphore_wait(barrier, 1 + size_p - 1 + size_z - 1)
    twin_copy(0).start()
    turned[...] = sign(rounds).T.reshape(turned.shape)

    def along_z(source, target, index):
        @pl.loop(1, size_z)
        def _(step):
            peer = (z + step) % size_z
            pltpu.make_async_remote_copy(
                src_ref=source.at[peer], dst_ref=target.at[z], send_sem=turn_send.at[index],
                recv_sem=turn_recv.at[index], device_id=on_ring(step), device_id_type=MESH,
            ).start()

        target[z] = source[z]

    along_z(turned, turned_in, 0)
    loads[-1].wait()
    lane = lax.broadcasted_iota(jnp.int32, (8, LANES), 1)
    table[0] = jnp.where(lane < count_ref[0], jnp.broadcast_to(rows[...], (8, LANES)), -1)

    @pl.loop(1, size_z)
    def _(step):
        pltpu.make_async_remote_copy(
            src_ref=table.at[0], dst_ref=table.at[step], send_sem=table_send.at[0], recv_sem=table_recv.at[0],
            device_id=on_ring(size_z - step), device_id_type=MESH,
        ).start()

    for chunk in range(1, rounds):
        signed[chunk] = sign(chunk)
        twin_copy(chunk).start()

    own_sign = (1 - 2 * core).astype(jnp.float32)

    def send_out(chunk):
        twin_copy(chunk).wait_recv()
        mixed[chunk] = (signed[chunk] * own_sign + other[chunk]).reshape(mixed.shape[1:])

        @pl.loop(1, size_p)
        def _(step):
            peer, device = in_plane(step)
            pltpu.make_async_remote_copy(
                src_ref=mixed.at[chunk, peer], dst_ref=spread.at[chunk, me],
                send_sem=out_send.at[chunk], recv_sem=out_recv.at[chunk],
                device_id=device, device_id_type=MESH,
            ).start()

        spread[chunk, me] = mixed[chunk, me]

    def turn_back(chunk):
        wait_bytes(spread.at[chunk, pl.ds(0, size_p - 1)], out_recv.at[chunk])
        values = butterflies([spread[chunk, source] for source in range(size_p)])
        for target in range(size_p):
            back[chunk, target] = values[target]

        @pl.loop(1, size_p)
        def _(step):
            peer, device = in_plane(step)
            pltpu.make_async_remote_copy(
                src_ref=back.at[chunk, peer], dst_ref=whole.at[chunk, me],
                send_sem=back_send.at[chunk], recv_sem=back_recv.at[chunk],
                device_id=device, device_id_type=MESH,
            ).start()

        whole[chunk, me] = back[chunk, me]

    def z_sign(step):
        return parity_sign(jnp.bitwise_and((z + step) % size_z, z), 4)

    def make_select():
        wait_bytes(table.at[pl.ds(1, size_z - 1)], table_recv.at[0])
        low = lax.broadcasted_iota(jnp.int32, (slots, LANES), 1)

        @pl.loop(0, size_z)
        def _(step):
            target = jnp.broadcast_to(table[step, 0:1, :].astype(jnp.float32), (LANES, slots)).T.astype(jnp.int32)
            sign = z_sign(step)
            base = parity_sign(jnp.bitwise_and(jnp.maximum(target, 0), low), 7)
            base = jnp.where(target < 0, 0.0, base * sign)
            blocks = [base]
            level = 7
            while len(blocks) * LANES < height:
                bit = jnp.bitwise_and(jnp.right_shift(jnp.maximum(target, 0), level), 1)
                flip = (1 - 2 * bit).astype(jnp.float32)
                blocks = blocks + [block * flip for block in blocks]
                level += 1
            for index, block in enumerate(blocks):
                select[step, :, index * LANES : (index + 1) * LANES] = block.astype(jnp.bfloat16)

    def make_terms(chunk):
        wait_bytes(whole.at[chunk, pl.ds(0, size_p - 1)], back_recv.at[chunk])
        value = whole[chunk].reshape(height, LANES)
        high = value.astype(jnp.bfloat16)
        rest = (value - high.astype(jnp.float32)).astype(jnp.bfloat16)
        both = jnp.concatenate([high, rest], axis=1)
        group = 4

        @pl.loop(0, size_z // group)
        def _(step):
            some = select[pl.ds(step * group, group)].reshape(group * slots, height)
            product = jnp.dot(some, both, preferred_element_type=jnp.float32)
            total = product[:, :LANES] + product[:, LANES:]
            terms[chunk, pl.ds(step * group, group)] = total.reshape(group, slots, LANES)

    half = size_z // 2

    def ways(chunk):
        longer = chunk % 2 == 0
        right = [(half if longer else half - 1) - i for i in range(half if longer else half - 1)]
        left = [(half + 1 if longer else half) + i for i in range(half - 1 if longer else half)]
        return right, left

    def ring_copy(chunk, way, step, term):
        return pltpu.make_async_remote_copy(
            src_ref=terms.at[chunk, term], dst_ref=ring.at[chunk, way, step],
            send_sem=ring_send.at[chunk, way, step], recv_sem=ring_recv.at[chunk, way, step],
            device_id=on_ring(1 if way == 0 else size_z - 1), device_id_type=MESH,
        )

    sent = []

    def ring_step(chunk, step):
        for way, targets in enumerate(ways(chunk)):
            if step > len(targets):
                continue
            term = targets[step] if step < len(targets) else 0
            if step > 0:
                ring_copy(chunk, way, step - 1, term).wait_recv()
                terms[chunk, term] = terms[chunk, term] + ring[chunk, way, step - 1]
            if step < len(targets):
                copy = ring_copy(chunk, way, step, term)
                copy.start()
                sent.append(copy)

    each = size_z // size_p

    def turned_to_plane():
        wait_bytes(turned_in.at[pl.ds(0, size_z - 1)], turn_recv.at[0])
        for target, value in enumerate(butterflies([turned_in[source] for source in range(size_z)])):
            turned_mid[target] = value
        turned_twin.start()

    def turned_out_to_plane():
        turned_twin.wait_recv()
        turned_mix[...] = turned_mid[...] * own_sign + turned_other[...]

        @pl.loop(1, size_p)
        def _(step):
            peer, device = in_plane(step)
            pltpu.make_async_remote_copy(
                src_ref=turned_mix.at[pl.ds(peer * each, each)], dst_ref=turned_spread.at[me],
                send_sem=turn_send.at[2], recv_sem=turn_recv.at[2], device_id=device, device_id_type=MESH,
            ).start()

        turned_spread[me] = turned_mix[pl.ds(me * each, each)]

    def turned_from_plane():
        wait_bytes(turned_spread.at[pl.ds(0, size_p - 1)], turn_recv.at[2])
        for target, value in enumerate(butterflies([turned_spread[source] for source in range(size_p)])):
            turned_back[target] = value

        @pl.loop(1, size_p)
        def _(step):
            peer, device = in_plane(step)
            pltpu.make_async_remote_copy(
                src_ref=turned_back.at[peer], dst_ref=turned_whole.at[pl.ds(me * each, each)],
                send_sem=turn_send.at[3], recv_sem=turn_recv.at[3], device_id=device, device_id_type=MESH,
            ).start()

        turned_whole[pl.ds(me * each, each)] = turned_back[me]

    def turned_select():
        wait_bytes(turned_whole.at[pl.ds(0, each * (size_p - 1))], turn_recv.at[3])
        deep = turned.shape[1]

        @pl.loop(0, size_z)
        def _(step):
            peer = (z + step) % size_z
            value = turned_whole[peer]
            high = value.astype(jnp.bfloat16).astype(jnp.float32)
            both = jnp.concatenate([high, value - high], axis=0).astype(jnp.bfloat16)
            product = lax.dot_general(
                both, select[step], (((1,), (1,)), ((), ())), preferred_element_type=jnp.float32
            )
            turned_out[peer] = (product[:deep] + product[deep:]) * z_sign(step)

        along_z(turned_out, turned_final, 4)

    turned_twin = pltpu.make_async_remote_copy(
        src_ref=turned_mid, dst_ref=turned_other, send_sem=turn_send.at[1], recv_sem=turn_recv.at[1],
        device_id=twin, device_id_type=MESH,
    )

    for chunk in range(rounds):
        send_out(chunk)
    turn_back(0)
    turn_back(1)
    make_select()
    turn_back(2)
    for chunk in range(rounds):
        make_terms(chunk)
        ring_step(chunk, 0)
    turned_to_plane()
    ring_step(0, 1)
    ring_step(1, 1)
    turned_out_to_plane()
    ring_step(2, 1)
    ring_step(0, 2)
    ring_step(1, 2)
    turned_from_plane()
    ring_step(2, 2)
    for step in range(3, half + 1):
        if step == 5:
            turned_select()
        for chunk in range(rounds):
            ring_step(chunk, step)
    if half < 5:
        turned_select()
    wait_bytes(turned_final.at[pl.ds(0, size_z - 1)], turn_recv.at[4])

    scale = 1.0 / math.sqrt(height * size_p * cores * size_z)
    pieces = [terms[chunk, 0] * scale for chunk in range(rounds)]
    pieces.append(turned_final[...].reshape(LANES, slots).T * scale)
    for chunk in range(chunks):
        sketch_ref[:, chunk * LANES : (chunk + 1) * LANES] = pieces[chunk]
    sketch = jnp.concatenate(pieces, axis=1)
    block = 0
    for i in range(chunks):
        product = jnp.dot(
            pieces[i].T, sketch[:, i * LANES :], precision=lax.Precision.HIGHEST, preferred_element_type=jnp.float32
        )
        for j in range(chunks - i):
            parts[block * LANES : (block + 1) * LANES, :] = product[:, j * LANES : (j + 1) * LANES]
            block += 1

    deep = sum_parts.shape[1]
    share = deep * size_p

    def twin_half(source, first, target, sem):
        return pltpu.make_async_remote_copy(
            src_ref=source.at[pl.ds(first, share)], dst_ref=target, send_sem=sum_send.at[sem],
            recv_sem=sum_recv.at[sem], device_id=twin, device_id_type=MESH,
        )

    mine = pl.multiple_of(core * share, 8)
    yours = pl.multiple_of((1 - core) * share, 8)
    first_swap = twin_half(parts, yours, half_parts, 0)
    first_swap.start()
    first_swap.wait_recv()
    half_parts[...] = half_parts[...] + parts[pl.ds(mine, share), :]

    @pl.loop(1, size_p)
    def _(step):
        peer, device = in_plane(step)
        pltpu.make_async_remote_copy(
            src_ref=half_parts.at[pl.ds(pl.multiple_of(peer * deep, 8), deep)], dst_ref=sum_parts.at[step - 1],
            send_sem=sum_send.at[1], recv_sem=sum_recv.at[1], device_id=device, device_id_type=MESH,
        ).start()

    total = half_parts[pl.ds(pl.multiple_of(me * deep, 8), deep), :]
    wait_bytes(sum_parts, sum_recv.at[1])
    for step in range(size_p - 1):
        total = total + sum_parts[step]

    low_size, high_size = z_low.shape[0], z_high.shape[0]
    z_lo, z_hi = z % low_size, z // low_size
    z_low[z_lo] = total
    for step in range(1, low_size):
        peer = z_hi * low_size + (z_lo + step) % low_size
        pltpu.make_async_remote_copy(
            src_ref=z_low.at[z_lo], dst_ref=z_low.at[z_lo], send_sem=sum_send.at[2], recv_sem=sum_recv.at[2],
            device_id=(peer * size_x + x, hi), device_id_type=MESH,
        ).start()
    wait_bytes(z_low.at[pl.ds(0, low_size - 1)], sum_recv.at[2])
    total = z_low[0]
    for step in range(1, low_size):
        total = total + z_low[step]
    z_high[z_hi] = total
    for step in range(1, high_size):
        peer = ((z_hi + step) % high_size) * low_size + z_lo
        pltpu.make_async_remote_copy(
            src_ref=z_high.at[z_hi], dst_ref=z_high.at[z_hi], send_sem=sum_send.at[3], recv_sem=sum_recv.at[3],
            device_id=(peer * size_x + x, hi), device_id_type=MESH,
        ).start()
    if high_size > 1:
        wait_bytes(z_high.at[pl.ds(0, high_size - 1)], sum_recv.at[3])
    total = z_high[0]
    for step in range(1, high_size):
        total = total + z_high[step]
    own = pl.ds(pl.multiple_of(core * share + me * deep, 8), deep)
    gathered[own, :] = total * (1.0 / (size_p * cores * size_z * slots))

    @pl.loop(1, size_p)
    def _(step):
        pltpu.make_async_remote_copy(
            src_ref=gathered.at[own], dst_ref=gathered.at[own], send_sem=sum_send.at[4], recv_sem=sum_recv.at[4],
            device_id=in_plane(step)[1], device_id_type=MESH,
        ).start()

    rest = pl.ds(0, deep * (size_p - 1))
    wait_bytes(gathered.at[rest], sum_recv.at[4])
    last_swap = twin_half(gathered, mine, gathered.at[pl.ds(mine, share)], 5)
    last_swap.start()
    last_swap.wait_recv()
    block = 0
    for i in range(chunks):
        for j in range(i, chunks):
            value = gathered[block * LANES : (block + 1) * LANES, :]
            gram_ref[i * LANES : (i + 1) * LANES, j * LANES : (j + 1) * LANES] = value
            if j > i:
                gram_ref[j * LANES : (j + 1) * LANES, i * LANES : (i + 1) * LANES] = value.T
            block += 1

    for copy in sent:
        copy.wait_send()
    wait_bytes(table.at[pl.ds(1, size_z - 1)], table_send.at[0])
    turned_twin.wait_send()
    wait_bytes(turned_in.at[pl.ds(0, size_z - 1)], turn_send.at[0])
    wait_bytes(turned_mix.at[pl.ds(0, each * (size_p - 1))], turn_send.at[2])
    wait_bytes(turned_back.at[pl.ds(0, size_p - 1)], turn_send.at[3])
    wait_bytes(turned_final.at[pl.ds(0, size_z - 1)], turn_send.at[4])
    for chunk in range(rounds):
        twin_copy(chunk).wait_send()
        wait_bytes(mixed.at[chunk, pl.ds(0, size_p - 1)], out_send.at[chunk])
        wait_bytes(back.at[chunk, pl.ds(0, size_p - 1)], back_send.at[chunk])
    first_swap.wait_send()
    wait_bytes(sum_parts, sum_send.at[1])
    wait_bytes(z_low.at[pl.ds(0, low_size - 1)], sum_send.at[2])
    if high_size > 1:
        wait_bytes(z_high.at[pl.ds(0, high_size - 1)], sum_send.at[3])
    wait_bytes(gathered.at[rest], sum_send.at[4])
    last_swap.wait_send()


def build(geo, matrix, sign_bits, sample_rows, sample_counts):
    size_z, size_x, size_hi = geo
    cores = 2
    size_p = size_x * size_hi // cores
    height, width = matrix.shape
    slots = sample_rows.shape[0]
    chunks = width // LANES
    packed = chunks * (chunks + 1) // 2 * LANES
    deep = packed // cores // size_p
    low_size = 4
    f32 = jnp.float32
    vmem = pl.BlockSpec(memory_space=pltpu.VMEM)
    hbm = pl.BlockSpec(memory_space=pltpu.HBM)
    dma = pltpu.SemaphoreType.DMA
    rounds = chunks - 1
    tall = (rounds, height, LANES)
    spread = (rounds, size_p, height // size_p, LANES)
    turned = (size_z, LANES // size_z, height)
    turned_spread = (size_p, size_z // size_p, LANES // size_z, height)
    turned_out = (size_z, LANES // size_z, slots)
    return pl.pallas_call(
        functools.partial(kernel, geo),
        out_shape=(
            jax.ShapeDtypeStruct((slots, width), f32),
            jax.ShapeDtypeStruct((width, width), f32),
        ),
        in_specs=[hbm, hbm, hbm, pl.BlockSpec(memory_space=pltpu.SMEM)],
        out_specs=(vmem, vmem),
        scratch_shapes=[
            pltpu.VMEM((chunks, height, LANES), f32),
            pltpu.VMEM(sign_bits.shape, jnp.int32),
            pltpu.VMEM((1, slots), jnp.int32),
            pltpu.VMEM(tall, f32),
            pltpu.VMEM(tall, f32),
            pltpu.VMEM(spread, f32),
            pltpu.VMEM(spread, f32),
            pltpu.VMEM(spread, f32),
            pltpu.VMEM(spread, f32),
            pltpu.VMEM((size_z, 8, LANES), jnp.int32),
            pltpu.VMEM((size_z, slots, height), jnp.bfloat16),
            pltpu.VMEM((rounds, size_z, slots, LANES), f32),
            pltpu.VMEM((rounds, 2, size_z // 2, slots, LANES), f32),
            pltpu.VMEM(turned, f32),
            pltpu.VMEM(turned, f32),
            pltpu.VMEM(turned, f32),
            pltpu.VMEM(turned, f32),
            pltpu.VMEM(turned, f32),
            pltpu.VMEM(turned_spread, f32),
            pltpu.VMEM(turned_spread, f32),
            pltpu.VMEM(turned, f32),
            pltpu.VMEM(turned_out, f32),
            pltpu.VMEM(turned_out, f32),

            pltpu.VMEM((packed, LANES), f32),
            pltpu.VMEM((packed // cores, LANES), f32),
            pltpu.VMEM((size_p - 1, deep, LANES), f32),
            pltpu.VMEM((low_size, deep, LANES), f32),
            pltpu.VMEM((size_z // low_size, deep, LANES), f32),
            pltpu.VMEM((packed, LANES), f32),
            dma((chunks + 2,)),
            dma((rounds,)),
            dma((rounds,)),
            dma((1,)),
            dma((1,)),
            dma((rounds,)),
            dma((rounds,)),
            dma((rounds,)),
            dma((rounds,)),
            dma((rounds, 2, size_z // 2)),
            dma((rounds, 2, size_z // 2)),
            dma((6,)),
            dma((6,)),
            dma((5,)),
            dma((5,)),
        ],
        compiler_params=pltpu.CompilerParams(
            collective_id=0, has_side_effects=True, vmem_limit_bytes=48 * 1024 * 1024
        ),
    )(matrix, sign_bits, sample_rows.reshape(1, slots), sample_counts)


def solution(mesh):
    size_x = 2
    geo = (mesh.shape["lo"] // size_x, size_x, mesh.shape["hi"])
    in_specs = (P(("lo", "hi"), None), P(None, ("lo", "hi")), P(("lo", "hi")), P(("lo", "hi")))
    out_specs = (P(("lo", "hi"), None), P())
    return jax.shard_map(
        functools.partial(build, geo), mesh=mesh, in_specs=in_specs, out_specs=out_specs, check_vma=False
    )
```

```python
import functools
import math

import jax
import jax.numpy as jnp
from jax import lax
from jax.experimental import pallas as pl
from jax.experimental.pallas import tpu as pltpu
from jax.sharding import PartitionSpec as P

MESH = pl.DeviceIdType.MESH
LANES = 128


def parity_sign(value, bits):
    shift = 1
    while shift < bits:
        shift *= 2
    while shift > 1:
        shift //= 2
        value = jnp.bitwise_xor(value, jnp.right_shift(value, shift))
    return (1 - 2 * jnp.bitwise_and(value, 1)).astype(jnp.float32)


def butterflies(values):
    stride = 1
    while stride < len(values):
        values = [
            values[i] + values[i + stride] if i // stride % 2 == 0 else values[i - stride] - values[i]
            for i in range(len(values))
        ]
        stride *= 2
    return values


def kernel(
    geo, matrix_ref, bits_ref, rows_ref, count_ref, sketch_ref, gram_ref,
    raw, bits, rows, signed, other, mixed, spread, back, whole, table, select, terms, ring,
    turned, turned_in, turned_mid, turned_other, turned_mix, turned_spread, turned_back, turned_whole, turned_out,
    turned_final, parts, half_parts, sum_parts, z_low, z_high, gathered,
    load_sem, core_send, core_recv, table_send, table_recv, out_send, out_recv, back_send, back_recv,
    ring_send, ring_recv, sum_send, sum_recv, turn_send, turn_recv,
):
    size_z, size_x, size_hi = geo
    cores = 2
    size_y = size_hi // cores
    size_p = size_x * size_y
    chunks = raw.shape[0]
    rounds = chunks - 1
    height = signed.shape[1]
    slots = terms.shape[2]
    panels = bits.shape[0]
    lo, hi = lax.axis_index("lo"), lax.axis_index("hi")
    z, x = lo // size_x, lo % size_x
    core = hi % cores
    me = x * size_y + hi // cores
    twin = (lo, hi + 1 - 2 * core)

    def in_plane(step):
        peer = (me + step) % size_p
        return peer, (z * size_x + peer // size_y, (peer % size_y) * cores + core)

    def on_ring(step):
        return (((z + step) % size_z) * size_x + x, hi)

    def wait_bytes(ref, sem):
        pltpu.make_async_copy(ref, ref, sem).wait()

    barrier = pltpu.get_barrier_semaphore()
    pl.semaphore_signal(barrier, inc=1, device_id=twin, device_id_type=MESH)

    @pl.loop(1, size_p)
    def _(step):
        pl.semaphore_signal(barrier, inc=1, device_id=in_plane(step)[1], device_id_type=MESH)

    @pl.loop(1, size_z)
    def _(step):
        pl.semaphore_signal(barrier, inc=1, device_id=on_ring(step), device_id_type=MESH)

    loads = [pltpu.make_async_copy(bits_ref, bits, load_sem.at[chunks])]
    for chunk in range(chunks):
        loads.append(pltpu.make_async_copy(
            matrix_ref.at[:, chunk * LANES : (chunk + 1) * LANES], raw.at[chunk], load_sem.at[chunk]
        ))
    loads.append(pltpu.make_async_copy(rows_ref, rows, load_sem.at[chunks + 1]))
    for load in loads:
        load.start()

    loads[0].wait()
    factors = (2 * bits[...] - 1).astype(jnp.float32)
    columns = [jnp.broadcast_to(factors[p : p + 1, :], (LANES, height)).T for p in range(panels)]

    def twin_copy(chunk):
        return pltpu.make_async_remote_copy(
            src_ref=signed.at[chunk], dst_ref=other.at[chunk], send_sem=core_send.at[chunk],
            recv_sem=core_recv.at[chunk], device_id=twin, device_id_type=MESH,
        )

    def sign(chunk):
        loads[1 + chunk].wait()
        return raw[chunk] * columns[chunk * panels // chunks]

    signed[0] = sign(0)
    loads[-1].wait()
    lane = lax.broadcasted_iota(jnp.int32, (8, LANES), 1)
    table[0] = jnp.where(lane < count_ref[0], jnp.broadcast_to(rows[...], (8, LANES)), -1)
    pl.semaphore_wait(barrier, 1 + size_p - 1 + size_z - 1)
    twin_copy(0).start()

    @pl.loop(1, size_z)
    def _(step):
        pltpu.make_async_remote_copy(
            src_ref=table.at[0], dst_ref=table.at[step], send_sem=table_send.at[0], recv_sem=table_recv.at[0],
            device_id=on_ring(size_z - step), device_id_type=MESH,
        ).start()

    turned[...] = sign(rounds).T.reshape(turned.shape)

    def along_z(source, target, index):
        @pl.loop(1, size_z)
        def _(step):
            peer = (z + step) % size_z
            pltpu.make_async_remote_copy(
                src_ref=source.at[peer], dst_ref=target.at[z], send_sem=turn_send.at[index],
                recv_sem=turn_recv.at[index], device_id=on_ring(step), device_id_type=MESH,
            ).start()

        target[z] = source[z]

    along_z(turned, turned_in, 0)
    for chunk in range(1, rounds):
        signed[chunk] = sign(chunk)
        twin_copy(chunk).start()

    own_sign = (1 - 2 * core).astype(jnp.float32)

    def send_out(chunk):
        twin_copy(chunk).wait_recv()
        mixed[chunk] = (signed[chunk] * own_sign + other[chunk]).reshape(mixed.shape[1:])

        @pl.loop(1, size_p)
        def _(step):
            peer, device = in_plane(step)
            pltpu.make_async_remote_copy(
                src_ref=mixed.at[chunk, peer], dst_ref=spread.at[chunk, me],
                send_sem=out_send.at[chunk], recv_sem=out_recv.at[chunk],
                device_id=device, device_id_type=MESH,
            ).start()

        spread[chunk, me] = mixed[chunk, me]

    def turn_back(chunk):
        wait_bytes(spread.at[chunk, pl.ds(0, size_p - 1)], out_recv.at[chunk])
        values = butterflies([spread[chunk, source] for source in range(size_p)])
        for target in range(size_p):
            back[chunk, target] = values[target]

        @pl.loop(1, size_p)
        def _(step):
            peer, device = in_plane(step)
            pltpu.make_async_remote_copy(
                src_ref=back.at[chunk, peer], dst_ref=whole.at[chunk, me],
                send_sem=back_send.at[chunk], recv_sem=back_recv.at[chunk],
                device_id=device, device_id_type=MESH,
            ).start()

        whole[chunk, me] = back[chunk, me]

    def z_sign(step):
        return parity_sign(jnp.bitwise_and((z + step) % size_z, z), 4)

    def make_select():
        wait_bytes(table.at[pl.ds(1, size_z - 1)], table_recv.at[0])
        low = lax.broadcasted_iota(jnp.int32, (slots, LANES), 1)

        @pl.loop(0, size_z)
        def _(step):
            target = jnp.broadcast_to(table[step, 0:1, :].astype(jnp.float32), (LANES, slots)).T.astype(jnp.int32)
            sign = z_sign(step)
            base = parity_sign(jnp.bitwise_and(jnp.maximum(target, 0), low), 7)
            base = jnp.where(target < 0, 0.0, base * sign)
            blocks = [base]
            level = 7
            while len(blocks) * LANES < height:
                bit = jnp.bitwise_and(jnp.right_shift(jnp.maximum(target, 0), level), 1)
                flip = (1 - 2 * bit).astype(jnp.float32)
                blocks = blocks + [block * flip for block in blocks]
                level += 1
            for index, block in enumerate(blocks):
                select[step, :, index * LANES : (index + 1) * LANES] = block.astype(jnp.bfloat16)

    def make_terms(chunk):
        wait_bytes(whole.at[chunk, pl.ds(0, size_p - 1)], back_recv.at[chunk])
        value = whole[chunk].reshape(height, LANES)
        high = value.astype(jnp.bfloat16)
        rest = (value - high.astype(jnp.float32)).astype(jnp.bfloat16)
        both = jnp.concatenate([high, rest], axis=1)
        group = 4

        @pl.loop(0, size_z // group)
        def _(step):
            some = select[pl.ds(step * group, group)].reshape(group * slots, height)
            product = jnp.dot(some, both, preferred_element_type=jnp.float32)
            total = product[:, :LANES] + product[:, LANES:]
            terms[chunk, pl.ds(step * group, group)] = total.reshape(group, slots, LANES)

    half = size_z // 2

    def ways(chunk):
        longer = chunk % 2 == 0
        right = [(half if longer else half - 1) - i for i in range(half if longer else half - 1)]
        left = [(half + 1 if longer else half) + i for i in range(half - 1 if longer else half)]
        return right, left

    def ring_copy(chunk, way, step, term):
        return pltpu.make_async_remote_copy(
            src_ref=terms.at[chunk, term], dst_ref=ring.at[chunk, way, step],
            send_sem=ring_send.at[chunk, way, step], recv_sem=ring_recv.at[chunk, way, step],
            device_id=on_ring(1 if way == 0 else size_z - 1), device_id_type=MESH,
        )

    sent = []

    def ring_step(chunk, step):
        for way, targets in enumerate(ways(chunk)):
            if step > len(targets):
                continue
            term = targets[step] if step < len(targets) else 0
            if step > 0:
                ring_copy(chunk, way, step - 1, term).wait_recv()
                terms[chunk, term] = terms[chunk, term] + ring[chunk, way, step - 1]
            if step < len(targets):
                copy = ring_copy(chunk, way, step, term)
                copy.start()
                sent.append(copy)

    each = size_z // size_p

    def turned_to_plane():
        wait_bytes(turned_in.at[pl.ds(0, size_z - 1)], turn_recv.at[0])
        for target, value in enumerate(butterflies([turned_in[source] for source in range(size_z)])):
            turned_mid[target] = value
        turned_twin.start()

    def turned_out_to_plane():
        turned_twin.wait_recv()
        turned_mix[...] = turned_mid[...] * own_sign + turned_other[...]

        @pl.loop(1, size_p)
        def _(step):
            peer, device = in_plane(step)
            pltpu.make_async_remote_copy(
                src_ref=turned_mix.at[pl.ds(peer * each, each)], dst_ref=turned_spread.at[me],
                send_sem=turn_send.at[2], recv_sem=turn_recv.at[2], device_id=device, device_id_type=MESH,
            ).start()

        turned_spread[me] = turned_mix[pl.ds(me * each, each)]

    def turned_from_plane():
        wait_bytes(turned_spread.at[pl.ds(0, size_p - 1)], turn_recv.at[2])
        for target, value in enumerate(butterflies([turned_spread[source] for source in range(size_p)])):
            turned_back[target] = value

        @pl.loop(1, size_p)
        def _(step):
            peer, device = in_plane(step)
            pltpu.make_async_remote_copy(
                src_ref=turned_back.at[peer], dst_ref=turned_whole.at[pl.ds(me * each, each)],
                send_sem=turn_send.at[3], recv_sem=turn_recv.at[3], device_id=device, device_id_type=MESH,
            ).start()

        turned_whole[pl.ds(me * each, each)] = turned_back[me]

    def turned_select():
        wait_bytes(turned_whole.at[pl.ds(0, each * (size_p - 1))], turn_recv.at[3])
        deep = turned.shape[1]

        @pl.loop(0, size_z)
        def _(step):
            peer = (z + step) % size_z
            value = turned_whole[peer]
            high = value.astype(jnp.bfloat16).astype(jnp.float32)
            both = jnp.concatenate([high, value - high], axis=0).astype(jnp.bfloat16)
            product = lax.dot_general(
                both, select[step], (((1,), (1,)), ((), ())), preferred_element_type=jnp.float32
            )
            turned_out[peer] = (product[:deep] + product[deep:]) * z_sign(step)

        along_z(turned_out, turned_final, 4)

    turned_twin = pltpu.make_async_remote_copy(
        src_ref=turned_mid, dst_ref=turned_other, send_sem=turn_send.at[1], recv_sem=turn_recv.at[1],
        device_id=twin, device_id_type=MESH,
    )

    for chunk in range(rounds):
        send_out(chunk)
    turn_back(0)
    make_select()
    turn_back(1)
    turn_back(2)
    for chunk in range(rounds):
        make_terms(chunk)
        ring_step(chunk, 0)
    turned_to_plane()
    ring_step(0, 1)
    ring_step(1, 1)
    turned_out_to_plane()
    ring_step(2, 1)
    ring_step(0, 2)
    ring_step(1, 2)
    turned_from_plane()
    ring_step(2, 2)
    for step in range(3, half + 1):
        if step == 5:
            turned_select()
        for chunk in range(rounds):
            ring_step(chunk, step)
    if half < 5:
        turned_select()
    wait_bytes(turned_final.at[pl.ds(0, size_z - 1)], turn_recv.at[4])

    scale = 1.0 / math.sqrt(height * size_p * cores * size_z)
    pieces = [terms[chunk, 0] * scale for chunk in range(rounds)]
    pieces.append(turned_final[...].reshape(LANES, slots).T * scale)
    for chunk in range(chunks):
        sketch_ref[:, chunk * LANES : (chunk + 1) * LANES] = pieces[chunk]
    sketch = jnp.concatenate(pieces, axis=1)
    block = 0
    for i in range(chunks):
        product = jnp.dot(
            pieces[i].T, sketch[:, i * LANES :], precision=lax.Precision.HIGHEST, preferred_element_type=jnp.float32
        )
        for j in range(chunks - i):
            parts[block * LANES : (block + 1) * LANES, :] = product[:, j * LANES : (j + 1) * LANES]
            block += 1

    deep = sum_parts.shape[1]
    share = deep * size_p

    def twin_half(source, first, target, sem):
        return pltpu.make_async_remote_copy(
            src_ref=source.at[pl.ds(first, share)], dst_ref=target, send_sem=sum_send.at[sem],
            recv_sem=sum_recv.at[sem], device_id=twin, device_id_type=MESH,
        )

    mine = pl.multiple_of(core * share, 8)
    yours = pl.multiple_of((1 - core) * share, 8)
    first_swap = twin_half(parts, yours, half_parts, 0)
    first_swap.start()
    first_swap.wait_recv()
    half_parts[...] = half_parts[...] + parts[pl.ds(mine, share), :]

    @pl.loop(1, size_p)
    def _(step):
        peer, device = in_plane(step)
        pltpu.make_async_remote_copy(
            src_ref=half_parts.at[pl.ds(pl.multiple_of(peer * deep, 8), deep)], dst_ref=sum_parts.at[step - 1],
            send_sem=sum_send.at[1], recv_sem=sum_recv.at[1], device_id=device, device_id_type=MESH,
        ).start()

    total = half_parts[pl.ds(pl.multiple_of(me * deep, 8), deep), :]
    wait_bytes(sum_parts, sum_recv.at[1])
    for step in range(size_p - 1):
        total = total + sum_parts[step]

    low_size, high_size = z_low.shape[0], z_high.shape[0]
    z_lo, z_hi = z % low_size, z // low_size
    z_low[z_lo] = total
    for step in range(1, low_size):
        peer = z_hi * low_size + (z_lo + step) % low_size
        pltpu.make_async_remote_copy(
            src_ref=z_low.at[z_lo], dst_ref=z_low.at[z_lo], send_sem=sum_send.at[2], recv_sem=sum_recv.at[2],
            device_id=(peer * size_x + x, hi), device_id_type=MESH,
        ).start()
    wait_bytes(z_low.at[pl.ds(0, low_size - 1)], sum_recv.at[2])
    total = z_low[0]
    for step in range(1, low_size):
        total = total + z_low[step]
    z_high[z_hi] = total
    for step in range(1, high_size):
        peer = ((z_hi + step) % high_size) * low_size + z_lo
        pltpu.make_async_remote_copy(
            src_ref=z_high.at[z_hi], dst_ref=z_high.at[z_hi], send_sem=sum_send.at[3], recv_sem=sum_recv.at[3],
            device_id=(peer * size_x + x, hi), device_id_type=MESH,
        ).start()
    if high_size > 1:
        wait_bytes(z_high.at[pl.ds(0, high_size - 1)], sum_recv.at[3])
    total = z_high[0]
    for step in range(1, high_size):
        total = total + z_high[step]
    own = pl.ds(pl.multiple_of(core * share + me * deep, 8), deep)
    gathered[own, :] = total * (1.0 / (size_p * cores * size_z * slots))

    @pl.loop(1, size_p)
    def _(step):
        pltpu.make_async_remote_copy(
            src_ref=gathered.at[own], dst_ref=gathered.at[own], send_sem=sum_send.at[4], recv_sem=sum_recv.at[4],
            device_id=in_plane(step)[1], device_id_type=MESH,
        ).start()

    rest = pl.ds(0, deep * (size_p - 1))
    wait_bytes(gathered.at[rest], sum_recv.at[4])
    last_swap = twin_half(gathered, mine, gathered.at[pl.ds(mine, share)], 5)
    last_swap.start()
    last_swap.wait_recv()
    block = 0
    for i in range(chunks):
        for j in range(i, chunks):
            value = gathered[block * LANES : (block + 1) * LANES, :]
            gram_ref[i * LANES : (i + 1) * LANES, j * LANES : (j + 1) * LANES] = value
            if j > i:
                gram_ref[j * LANES : (j + 1) * LANES, i * LANES : (i + 1) * LANES] = value.T
            block += 1

    for copy in sent:
        copy.wait_send()
    wait_bytes(table.at[pl.ds(1, size_z - 1)], table_send.at[0])
    turned_twin.wait_send()
    wait_bytes(turned_in.at[pl.ds(0, size_z - 1)], turn_send.at[0])
    wait_bytes(turned_mix.at[pl.ds(0, each * (size_p - 1))], turn_send.at[2])
    wait_bytes(turned_back.at[pl.ds(0, size_p - 1)], turn_send.at[3])
    wait_bytes(turned_final.at[pl.ds(0, size_z - 1)], turn_send.at[4])
    for chunk in range(rounds):
        twin_copy(chunk).wait_send()
        wait_bytes(mixed.at[chunk, pl.ds(0, size_p - 1)], out_send.at[chunk])
        wait_bytes(back.at[chunk, pl.ds(0, size_p - 1)], back_send.at[chunk])
    first_swap.wait_send()
    wait_bytes(sum_parts, sum_send.at[1])
    wait_bytes(z_low.at[pl.ds(0, low_size - 1)], sum_send.at[2])
    if high_size > 1:
        wait_bytes(z_high.at[pl.ds(0, high_size - 1)], sum_send.at[3])
    wait_bytes(gathered.at[rest], sum_send.at[4])
    last_swap.wait_send()


def build(geo, matrix, sign_bits, sample_rows, sample_counts):
    size_z, size_x, size_hi = geo
    cores = 2
    size_p = size_x * size_hi // cores
    height, width = matrix.shape
    slots = sample_rows.shape[0]
    chunks = width // LANES
    packed = chunks * (chunks + 1) // 2 * LANES
    deep = packed // cores // size_p
    low_size = 4
    f32 = jnp.float32
    vmem = pl.BlockSpec(memory_space=pltpu.VMEM)
    hbm = pl.BlockSpec(memory_space=pltpu.HBM)
    dma = pltpu.SemaphoreType.DMA
    rounds = chunks - 1
    tall = (rounds, height, LANES)
    spread = (rounds, size_p, height // size_p, LANES)
    turned = (size_z, LANES // size_z, height)
    turned_spread = (size_p, size_z // size_p, LANES // size_z, height)
    turned_out = (size_z, LANES // size_z, slots)
    return pl.pallas_call(
        functools.partial(kernel, geo),
        out_shape=(
            jax.ShapeDtypeStruct((slots, width), f32),
            jax.ShapeDtypeStruct((width, width), f32),
        ),
        in_specs=[hbm, hbm, hbm, pl.BlockSpec(memory_space=pltpu.SMEM)],
        out_specs=(vmem, vmem),
        scratch_shapes=[
            pltpu.VMEM((chunks, height, LANES), f32),
            pltpu.VMEM(sign_bits.shape, jnp.int32),
            pltpu.VMEM((1, slots), jnp.int32),
            pltpu.VMEM(tall, f32),
            pltpu.VMEM(tall, f32),
            pltpu.VMEM(spread, f32),
            pltpu.VMEM(spread, f32),
            pltpu.VMEM(spread, f32),
            pltpu.VMEM(spread, f32),
            pltpu.VMEM((size_z, 8, LANES), jnp.int32),
            pltpu.VMEM((size_z, slots, height), jnp.bfloat16),
            pltpu.VMEM((rounds, size_z, slots, LANES), f32),
            pltpu.VMEM((rounds, 2, size_z // 2, slots, LANES), f32),
            pltpu.VMEM(turned, f32),
            pltpu.VMEM(turned, f32),
            pltpu.VMEM(turned, f32),
            pltpu.VMEM(turned, f32),
            pltpu.VMEM(turned, f32),
            pltpu.VMEM(turned_spread, f32),
            pltpu.VMEM(turned_spread, f32),
            pltpu.VMEM(turned, f32),
            pltpu.VMEM(turned_out, f32),
            pltpu.VMEM(turned_out, f32),

            pltpu.VMEM((packed, LANES), f32),
            pltpu.VMEM((packed // cores, LANES), f32),
            pltpu.VMEM((size_p - 1, deep, LANES), f32),
            pltpu.VMEM((low_size, deep, LANES), f32),
            pltpu.VMEM((size_z // low_size, deep, LANES), f32),
            pltpu.VMEM((packed, LANES), f32),
            dma((chunks + 2,)),
            dma((rounds,)),
            dma((rounds,)),
            dma((1,)),
            dma((1,)),
            dma((rounds,)),
            dma((rounds,)),
            dma((rounds,)),
            dma((rounds,)),
            dma((rounds, 2, size_z // 2)),
            dma((rounds, 2, size_z // 2)),
            dma((6,)),
            dma((6,)),
            dma((5,)),
            dma((5,)),
        ],
        compiler_params=pltpu.CompilerParams(
            collective_id=0, has_side_effects=True, vmem_limit_bytes=48 * 1024 * 1024
        ),
    )(matrix, sign_bits, sample_rows.reshape(1, slots), sample_counts)


def solution(mesh):
    size_x = 2
    geo = (mesh.shape["lo"] // size_x, size_x, mesh.shape["hi"])
    in_specs = (P(("lo", "hi"), None), P(None, ("lo", "hi")), P(("lo", "hi")), P(("lo", "hi")))
    out_specs = (P(("lo", "hi"), None), P())
    return jax.shard_map(
        functools.partial(build, geo), mesh=mesh, in_specs=in_specs, out_specs=out_specs, check_vma=False
    )
```

```python
import functools
import math

import jax
import jax.numpy as jnp
from jax import lax
from jax.experimental import pallas as pl
from jax.experimental.pallas import tpu as pltpu
from jax.sharding import PartitionSpec as P

MESH = pl.DeviceIdType.MESH
LANES = 128


def parity_sign(value, bits):
    shift = 1
    while shift < bits:
        shift *= 2
    while shift > 1:
        shift //= 2
        value = jnp.bitwise_xor(value, jnp.right_shift(value, shift))
    return (1 - 2 * jnp.bitwise_and(value, 1)).astype(jnp.float32)


def butterflies(values):
    stride = 1
    while stride < len(values):
        values = [
            values[i] + values[i + stride] if i // stride % 2 == 0 else values[i - stride] - values[i]
            for i in range(len(values))
        ]
        stride *= 2
    return values


def kernel(
    geo, matrix_ref, bits_ref, rows_ref, count_ref, sketch_ref, gram_ref,
    raw, bits, rows, signed, other, mixed, spread, back, whole, table, select, terms, ring,
    turned, turned_in, turned_mid, turned_other, turned_mix, turned_spread, turned_back, turned_whole, turned_out,
    turned_final, parts, half_parts, sum_parts, z_low, z_high, gathered,
    load_sem, core_send, core_recv, table_send, table_recv, out_send, out_recv, back_send, back_recv,
    ring_send, ring_recv, sum_send, sum_recv, turn_send, turn_recv,
):
    size_z, size_x, size_hi = geo
    cores = 2
    size_y = size_hi // cores
    size_p = size_x * size_y
    chunks = raw.shape[0]
    rounds = chunks - 1
    height = signed.shape[1]
    slots = terms.shape[2]
    panels = bits.shape[0]
    lo, hi = lax.axis_index("lo"), lax.axis_index("hi")
    z, x = lo // size_x, lo % size_x
    core = hi % cores
    me = x * size_y + hi // cores
    twin = (lo, hi + 1 - 2 * core)

    def in_plane(step):
        peer = (me + step) % size_p
        return peer, (z * size_x + peer // size_y, (peer % size_y) * cores + core)

    def on_ring(step):
        return (((z + step) % size_z) * size_x + x, hi)

    def wait_bytes(ref, sem):
        pltpu.make_async_copy(ref, ref, sem).wait()

    barrier = pltpu.get_barrier_semaphore()
    pl.semaphore_signal(barrier, inc=1, device_id=twin, device_id_type=MESH)

    @pl.loop(1, size_p)
    def _(step):
        pl.semaphore_signal(barrier, inc=1, device_id=in_plane(step)[1], device_id_type=MESH)

    @pl.loop(1, size_z)
    def _(step):
        pl.semaphore_signal(barrier, inc=1, device_id=on_ring(step), device_id_type=MESH)

    loads = [pltpu.make_async_copy(bits_ref, bits, load_sem.at[chunks])]
    for chunk in range(chunks):
        loads.append(pltpu.make_async_copy(
            matrix_ref.at[:, chunk * LANES : (chunk + 1) * LANES], raw.at[chunk], load_sem.at[chunk]
        ))
    loads.append(pltpu.make_async_copy(rows_ref, rows, load_sem.at[chunks + 1]))
    for load in loads:
        load.start()

    loads[0].wait()
    factors = (2 * bits[...] - 1).astype(jnp.float32)
    columns = {}

    def column(panel):
        if panel not in columns:
            columns[panel] = jnp.broadcast_to(factors[panel : panel + 1, :], (LANES, height)).T
        return columns[panel]

    def twin_copy(chunk):
        return pltpu.make_async_remote_copy(
            src_ref=signed.at[chunk], dst_ref=other.at[chunk], send_sem=core_send.at[chunk],
            recv_sem=core_recv.at[chunk], device_id=twin, device_id_type=MESH,
        )

    def sign(chunk):
        loads[1 + chunk].wait()
        return raw[chunk] * column(chunk * panels // chunks)

    signed[0] = sign(0)
    loads[-1].wait()
    lane = lax.broadcasted_iota(jnp.int32, (8, LANES), 1)
    table[0] = jnp.where(lane < count_ref[0], jnp.broadcast_to(rows[...], (8, LANES)), -1)
    pl.semaphore_wait(barrier, 1 + size_p - 1 + size_z - 1)
    twin_copy(0).start()

    @pl.loop(1, size_z)
    def _(step):
        pltpu.make_async_remote_copy(
            src_ref=table.at[0], dst_ref=table.at[step], send_sem=table_send.at[0], recv_sem=table_recv.at[0],
            device_id=on_ring(size_z - step), device_id_type=MESH,
        ).start()

    turned[...] = sign(rounds).T.reshape(turned.shape)

    def along_z(source, target, index):
        @pl.loop(1, size_z)
        def _(step):
            peer = (z + step) % size_z
            pltpu.make_async_remote_copy(
                src_ref=source.at[peer], dst_ref=target.at[z], send_sem=turn_send.at[index],
                recv_sem=turn_recv.at[index], device_id=on_ring(step), device_id_type=MESH,
            ).start()

        target[z] = source[z]

    along_z(turned, turned_in, 0)
    own_sign = (1 - 2 * core).astype(jnp.float32)

    def send_out(chunk):
        twin_copy(chunk).wait_recv()
        mixed[chunk] = (signed[chunk] * own_sign + other[chunk]).reshape(mixed.shape[1:])

        @pl.loop(1, size_p)
        def _(step):
            peer, device = in_plane(step)
            pltpu.make_async_remote_copy(
                src_ref=mixed.at[chunk, peer], dst_ref=spread.at[chunk, me],
                send_sem=out_send.at[chunk], recv_sem=out_recv.at[chunk],
                device_id=device, device_id_type=MESH,
            ).start()

        spread[chunk, me] = mixed[chunk, me]

    def turn_back(chunk):
        wait_bytes(spread.at[chunk, pl.ds(0, size_p - 1)], out_recv.at[chunk])
        values = butterflies([spread[chunk, source] for source in range(size_p)])
        for target in range(size_p):
            back[chunk, target] = values[target]

        @pl.loop(1, size_p)
        def _(step):
            peer, device = in_plane(step)
            pltpu.make_async_remote_copy(
                src_ref=back.at[chunk, peer], dst_ref=whole.at[chunk, me],
                send_sem=back_send.at[chunk], recv_sem=back_recv.at[chunk],
                device_id=device, device_id_type=MESH,
            ).start()

        whole[chunk, me] = back[chunk, me]

    def z_sign(step):
        return parity_sign(jnp.bitwise_and((z + step) % size_z, z), 4)

    def make_select():
        wait_bytes(table.at[pl.ds(1, size_z - 1)], table_recv.at[0])
        low = lax.broadcasted_iota(jnp.int32, (slots, LANES), 1)

        @pl.loop(0, size_z)
        def _(step):
            target = jnp.broadcast_to(table[step, 0:1, :].astype(jnp.float32), (LANES, slots)).T.astype(jnp.int32)
            sign = z_sign(step)
            base = parity_sign(jnp.bitwise_and(jnp.maximum(target, 0), low), 7)
            base = jnp.where(target < 0, 0.0, base * sign)
            blocks = [base]
            level = 7
            while len(blocks) * LANES < height:
                bit = jnp.bitwise_and(jnp.right_shift(jnp.maximum(target, 0), level), 1)
                flip = (1 - 2 * bit).astype(jnp.float32)
                blocks = blocks + [block * flip for block in blocks]
                level += 1
            for index, block in enumerate(blocks):
                select[step, :, index * LANES : (index + 1) * LANES] = block.astype(jnp.bfloat16)

    def make_terms(chunk):
        wait_bytes(whole.at[chunk, pl.ds(0, size_p - 1)], back_recv.at[chunk])
        value = whole[chunk].reshape(height, LANES)
        high = value.astype(jnp.bfloat16)
        rest = (value - high.astype(jnp.float32)).astype(jnp.bfloat16)
        both = jnp.concatenate([high, rest], axis=1)
        group = 4

        @pl.loop(0, size_z // group)
        def _(step):
            some = select[pl.ds(step * group, group)].reshape(group * slots, height)
            product = jnp.dot(some, both, preferred_element_type=jnp.float32)
            total = product[:, :LANES] + product[:, LANES:]
            terms[chunk, pl.ds(step * group, group)] = total.reshape(group, slots, LANES)

    half = size_z // 2

    def ways(chunk):
        longer = chunk % 2 == 0
        right = [(half if longer else half - 1) - i for i in range(half if longer else half - 1)]
        left = [(half + 1 if longer else half) + i for i in range(half - 1 if longer else half)]
        return right, left

    def ring_copy(chunk, way, step, term):
        return pltpu.make_async_remote_copy(
            src_ref=terms.at[chunk, term], dst_ref=ring.at[chunk, way, step],
            send_sem=ring_send.at[chunk, way, step], recv_sem=ring_recv.at[chunk, way, step],
            device_id=on_ring(1 if way == 0 else size_z - 1), device_id_type=MESH,
        )

    sent = []

    def ring_step(chunk, step):
        for way, targets in enumerate(ways(chunk)):
            if step > len(targets):
                continue
            term = targets[step] if step < len(targets) else 0
            if step > 0:
                ring_copy(chunk, way, step - 1, term).wait_recv()
                terms[chunk, term] = terms[chunk, term] + ring[chunk, way, step - 1]
            if step < len(targets):
                copy = ring_copy(chunk, way, step, term)
                copy.start()
                sent.append(copy)

    each = size_z // size_p

    def turned_to_plane():
        wait_bytes(turned_in.at[pl.ds(0, size_z - 1)], turn_recv.at[0])
        for target, value in enumerate(butterflies([turned_in[source] for source in range(size_z)])):
            turned_mid[target] = value
        turned_twin.start()

    def turned_out_to_plane():
        turned_twin.wait_recv()
        turned_mix[...] = turned_mid[...] * own_sign + turned_other[...]

        @pl.loop(1, size_p)
        def _(step):
            peer, device = in_plane(step)
            pltpu.make_async_remote_copy(
                src_ref=turned_mix.at[pl.ds(peer * each, each)], dst_ref=turned_spread.at[me],
                send_sem=turn_send.at[2], recv_sem=turn_recv.at[2], device_id=device, device_id_type=MESH,
            ).start()

        turned_spread[me] = turned_mix[pl.ds(me * each, each)]

    def turned_from_plane():
        wait_bytes(turned_spread.at[pl.ds(0, size_p - 1)], turn_recv.at[2])
        for target, value in enumerate(butterflies([turned_spread[source] for source in range(size_p)])):
            turned_back[target] = value

        @pl.loop(1, size_p)
        def _(step):
            peer, device = in_plane(step)
            pltpu.make_async_remote_copy(
                src_ref=turned_back.at[peer], dst_ref=turned_whole.at[pl.ds(me * each, each)],
                send_sem=turn_send.at[3], recv_sem=turn_recv.at[3], device_id=device, device_id_type=MESH,
            ).start()

        turned_whole[pl.ds(me * each, each)] = turned_back[me]

    def turned_select():
        wait_bytes(turned_whole.at[pl.ds(0, each * (size_p - 1))], turn_recv.at[3])
        deep = turned.shape[1]

        @pl.loop(0, size_z)
        def _(step):
            peer = (z + step) % size_z
            value = turned_whole[peer]
            high = value.astype(jnp.bfloat16).astype(jnp.float32)
            both = jnp.concatenate([high, value - high], axis=0).astype(jnp.bfloat16)
            product = lax.dot_general(
                both, select[step], (((1,), (1,)), ((), ())), preferred_element_type=jnp.float32
            )
            turned_out[peer] = (product[:deep] + product[deep:]) * z_sign(step)

        along_z(turned_out, turned_final, 4)

    turned_twin = pltpu.make_async_remote_copy(
        src_ref=turned_mid, dst_ref=turned_other, send_sem=turn_send.at[1], recv_sem=turn_recv.at[1],
        device_id=twin, device_id_type=MESH,
    )

    send_out(0)
    for chunk in range(1, rounds):
        signed[chunk] = sign(chunk)
        twin_copy(chunk).start()
    for chunk in range(1, rounds):
        send_out(chunk)
    turn_back(0)
    make_select()
    turn_back(1)
    turn_back(2)
    for chunk in range(rounds):
        make_terms(chunk)
        ring_step(chunk, 0)
    turned_to_plane()
    ring_step(0, 1)
    ring_step(1, 1)
    turned_out_to_plane()
    ring_step(2, 1)
    ring_step(0, 2)
    ring_step(1, 2)
    turned_from_plane()
    ring_step(2, 2)
    for step in range(3, half + 1):
        if step == 5:
            turned_select()
        for chunk in range(rounds):
            ring_step(chunk, step)
    if half < 5:
        turned_select()
    wait_bytes(turned_final.at[pl.ds(0, size_z - 1)], turn_recv.at[4])

    scale = 1.0 / math.sqrt(height * size_p * cores * size_z)
    pieces = [terms[chunk, 0] * scale for chunk in range(rounds)]
    pieces.append(turned_final[...].reshape(LANES, slots).T * scale)
    for chunk in range(chunks):
        sketch_ref[:, chunk * LANES : (chunk + 1) * LANES] = pieces[chunk]
    sketch = jnp.concatenate(pieces, axis=1)
    block = 0
    for i in range(chunks):
        product = jnp.dot(
            pieces[i].T, sketch[:, i * LANES :], precision=lax.Precision.HIGHEST, preferred_element_type=jnp.float32
        )
        for j in range(chunks - i):
            parts[block * LANES : (block + 1) * LANES, :] = product[:, j * LANES : (j + 1) * LANES]
            block += 1

    deep = sum_parts.shape[1]
    share = deep * size_p

    def twin_half(source, first, target, sem):
        return pltpu.make_async_remote_copy(
            src_ref=source.at[pl.ds(first, share)], dst_ref=target, send_sem=sum_send.at[sem],
            recv_sem=sum_recv.at[sem], device_id=twin, device_id_type=MESH,
        )

    mine = pl.multiple_of(core * share, 8)
    yours = pl.multiple_of((1 - core) * share, 8)
    first_swap = twin_half(parts, yours, half_parts, 0)
    first_swap.start()
    first_swap.wait_recv()
    half_parts[...] = half_parts[...] + parts[pl.ds(mine, share), :]

    @pl.loop(1, size_p)
    def _(step):
        peer, device = in_plane(step)
        pltpu.make_async_remote_copy(
            src_ref=half_parts.at[pl.ds(pl.multiple_of(peer * deep, 8), deep)], dst_ref=sum_parts.at[step - 1],
            send_sem=sum_send.at[1], recv_sem=sum_recv.at[1], device_id=device, device_id_type=MESH,
        ).start()

    total = half_parts[pl.ds(pl.multiple_of(me * deep, 8), deep), :]
    wait_bytes(sum_parts, sum_recv.at[1])
    for step in range(size_p - 1):
        total = total + sum_parts[step]

    low_size, high_size = z_low.shape[0], z_high.shape[0]
    z_lo, z_hi = z % low_size, z // low_size
    z_low[z_lo] = total
    for step in range(1, low_size):
        peer = z_hi * low_size + (z_lo + step) % low_size
        pltpu.make_async_remote_copy(
            src_ref=z_low.at[z_lo], dst_ref=z_low.at[z_lo], send_sem=sum_send.at[2], recv_sem=sum_recv.at[2],
            device_id=(peer * size_x + x, hi), device_id_type=MESH,
        ).start()
    wait_bytes(z_low.at[pl.ds(0, low_size - 1)], sum_recv.at[2])
    total = z_low[0]
    for step in range(1, low_size):
        total = total + z_low[step]
    z_high[z_hi] = total
    for step in range(1, high_size):
        peer = ((z_hi + step) % high_size) * low_size + z_lo
        pltpu.make_async_remote_copy(
            src_ref=z_high.at[z_hi], dst_ref=z_high.at[z_hi], send_sem=sum_send.at[3], recv_sem=sum_recv.at[3],
            device_id=(peer * size_x + x, hi), device_id_type=MESH,
        ).start()
    if high_size > 1:
        wait_bytes(z_high.at[pl.ds(0, high_size - 1)], sum_recv.at[3])
    total = z_high[0]
    for step in range(1, high_size):
        total = total + z_high[step]
    own = pl.ds(pl.multiple_of(core * share + me * deep, 8), deep)
    gathered[own, :] = total * (1.0 / (size_p * cores * size_z * slots))

    @pl.loop(1, size_p)
    def _(step):
        pltpu.make_async_remote_copy(
            src_ref=gathered.at[own], dst_ref=gathered.at[own], send_sem=sum_send.at[4], recv_sem=sum_recv.at[4],
            device_id=in_plane(step)[1], device_id_type=MESH,
        ).start()

    rest = pl.ds(0, deep * (size_p - 1))
    wait_bytes(gathered.at[rest], sum_recv.at[4])
    last_swap = twin_half(gathered, mine, gathered.at[pl.ds(mine, share)], 5)
    last_swap.start()
    last_swap.wait_recv()
    block = 0
    for i in range(chunks):
        for j in range(i, chunks):
            value = gathered[block * LANES : (block + 1) * LANES, :]
            gram_ref[i * LANES : (i + 1) * LANES, j * LANES : (j + 1) * LANES] = value
            if j > i:
                gram_ref[j * LANES : (j + 1) * LANES, i * LANES : (i + 1) * LANES] = value.T
            block += 1

    for copy in sent:
        copy.wait_send()
    wait_bytes(table.at[pl.ds(1, size_z - 1)], table_send.at[0])
    turned_twin.wait_send()
    wait_bytes(turned_in.at[pl.ds(0, size_z - 1)], turn_send.at[0])
    wait_bytes(turned_mix.at[pl.ds(0, each * (size_p - 1))], turn_send.at[2])
    wait_bytes(turned_back.at[pl.ds(0, size_p - 1)], turn_send.at[3])
    wait_bytes(turned_final.at[pl.ds(0, size_z - 1)], turn_send.at[4])
    for chunk in range(rounds):
        twin_copy(chunk).wait_send()
        wait_bytes(mixed.at[chunk, pl.ds(0, size_p - 1)], out_send.at[chunk])
        wait_bytes(back.at[chunk, pl.ds(0, size_p - 1)], back_send.at[chunk])
    first_swap.wait_send()
    wait_bytes(sum_parts, sum_send.at[1])
    wait_bytes(z_low.at[pl.ds(0, low_size - 1)], sum_send.at[2])
    if high_size > 1:
        wait_bytes(z_high.at[pl.ds(0, high_size - 1)], sum_send.at[3])
    wait_bytes(gathered.at[rest], sum_send.at[4])
    last_swap.wait_send()


def build(geo, matrix, sign_bits, sample_rows, sample_counts):
    size_z, size_x, size_hi = geo
    cores = 2
    size_p = size_x * size_hi // cores
    height, width = matrix.shape
    slots = sample_rows.shape[0]
    chunks = width // LANES
    packed = chunks * (chunks + 1) // 2 * LANES
    deep = packed // cores // size_p
    low_size = 4
    f32 = jnp.float32
    vmem = pl.BlockSpec(memory_space=pltpu.VMEM)
    hbm = pl.BlockSpec(memory_space=pltpu.HBM)
    dma = pltpu.SemaphoreType.DMA
    rounds = chunks - 1
    tall = (rounds, height, LANES)
    spread = (rounds, size_p, height // size_p, LANES)
    turned = (size_z, LANES // size_z, height)
    turned_spread = (size_p, size_z // size_p, LANES // size_z, height)
    turned_out = (size_z, LANES // size_z, slots)
    return pl.pallas_call(
        functools.partial(kernel, geo),
        out_shape=(
            jax.ShapeDtypeStruct((slots, width), f32),
            jax.ShapeDtypeStruct((width, width), f32),
        ),
        in_specs=[hbm, hbm, hbm, pl.BlockSpec(memory_space=pltpu.SMEM)],
        out_specs=(vmem, vmem),
        scratch_shapes=[
            pltpu.VMEM((chunks, height, LANES), f32),
            pltpu.VMEM(sign_bits.shape, jnp.int32),
            pltpu.VMEM((1, slots), jnp.int32),
            pltpu.VMEM(tall, f32),
            pltpu.VMEM(tall, f32),
            pltpu.VMEM(spread, f32),
            pltpu.VMEM(spread, f32),
            pltpu.VMEM(spread, f32),
            pltpu.VMEM(spread, f32),
            pltpu.VMEM((size_z, 8, LANES), jnp.int32),
            pltpu.VMEM((size_z, slots, height), jnp.bfloat16),
            pltpu.VMEM((rounds, size_z, slots, LANES), f32),
            pltpu.VMEM((rounds, 2, size_z // 2, slots, LANES), f32),
            pltpu.VMEM(turned, f32),
            pltpu.VMEM(turned, f32),
            pltpu.VMEM(turned, f32),
            pltpu.VMEM(turned, f32),
            pltpu.VMEM(turned, f32),
            pltpu.VMEM(turned_spread, f32),
            pltpu.VMEM(turned_spread, f32),
            pltpu.VMEM(turned, f32),
            pltpu.VMEM(turned_out, f32),
            pltpu.VMEM(turned_out, f32),

            pltpu.VMEM((packed, LANES), f32),
            pltpu.VMEM((packed // cores, LANES), f32),
            pltpu.VMEM((size_p - 1, deep, LANES), f32),
            pltpu.VMEM((low_size, deep, LANES), f32),
            pltpu.VMEM((size_z // low_size, deep, LANES), f32),
            pltpu.VMEM((packed, LANES), f32),
            dma((chunks + 2,)),
            dma((rounds,)),
            dma((rounds,)),
            dma((1,)),
            dma((1,)),
            dma((rounds,)),
            dma((rounds,)),
            dma((rounds,)),
            dma((rounds,)),
            dma((rounds, 2, size_z // 2)),
            dma((rounds, 2, size_z // 2)),
            dma((6,)),
            dma((6,)),
            dma((5,)),
            dma((5,)),
        ],
        compiler_params=pltpu.CompilerParams(
            collective_id=0, has_side_effects=True, vmem_limit_bytes=48 * 1024 * 1024
        ),
    )(matrix, sign_bits, sample_rows.reshape(1, slots), sample_counts)


def solution(mesh):
    size_x = 2
    geo = (mesh.shape["lo"] // size_x, size_x, mesh.shape["hi"])
    in_specs = (P(("lo", "hi"), None), P(None, ("lo", "hi")), P(("lo", "hi")), P(("lo", "hi")))
    out_specs = (P(("lo", "hi"), None), P())
    return jax.shard_map(
        functools.partial(build, geo), mesh=mesh, in_specs=in_specs, out_specs=out_specs, check_vma=False
    )
```
